256 devices in a mesh: ctx: 4 (over z_hi, core), exp: 64 (over x, y, z_lo).
Axes of the slice: x: 4, y: 4, z: 8 (z_hi: 2, z_lo: 4; z = z_hi * 4 + z_lo), core: 2. Of those that a mesh axis runs over, the one named last changes fastest.
Arguments:
- query: bfloat16 [64, 512, 1024], P('exp', 'ctx'), may hold values from -6 to 6
- key_states: bfloat16 [64, 512, 1024], P('exp', 'ctx'), may hold values from -6 to 6
- value_states: bfloat16 [64, 512, 1024], P('exp', 'ctx'), may hold values from -6 to 6
- segment_ids: int32 [64, 512], P('exp', 'ctx'), may hold values from 0 to 7, never falling along the last dimension, each value on 1 to 256 neighbouring positions
- out_weight: bfloat16 [1024, 2048], P('ctx'), may hold values from -0.1875 to 0.1875
- grad_out: bfloat16 [64, 512, 2048], P('exp', 'ctx'), may hold values from -6 to 6
- routes: int32 [64, 512, 4], P('exp', 'ctx'), may hold values from 0 to 63, all different within a row; in each aligned block of 128 rows (0 to 127, 128 to 255, ..., all dimensions but the last counted through in order) at most 10 rows name the same one
- route_gates: float32 [64, 512, 4], P('exp', 'ctx'), may hold values from 0.05 to 0.6
- w_gate: bfloat16 [64, 2048, 1408], P('exp', None, 'ctx'), may hold values from -0.125 to 0.125
- w_up: bfloat16 [64, 2048, 1408], P('exp', None, 'ctx'), may hold values from -0.125 to 0.125
- w_down: bfloat16 [64, 2048, 1408], P('exp', None, 'ctx'), may hold values from -0.15625 to 0.15625
- saved_gate: bfloat16 [64, 2560, 1408], P('exp', 'ctx'), may hold values from -8 to 8
- saved_up: bfloat16 [64, 2560, 1408], P('exp', 'ctx'), may hold values from -8 to 8
Outputs:
- d_hidden: bfloat16 [64, 512, 2048], P('exp', 'ctx')
- grad_query: bfloat16 [64, 512, 1024], P('exp', 'ctx')
- grad_key: bfloat16 [64, 512, 1024], P('exp', 'ctx')
- grad_value: bfloat16 [64, 512, 1024], P('exp', 'ctx')
The draws below stay inside these ranges and needn't reach their ends.
Inputs may be any that keep to these rules, and one draw needn't show every extreme that they name: `routes`: each position names 4 different experts; within the 128 positions of one device no expert is named more than 10 times. `segment_ids`: never falling along a sequence; a segment covers 1 to 256 positions.
All inputs are finite; a program needn't handle non-finite values.
Results may differ from the reference program's by a relative error of at most 0.018.
Values may be sent and summed in bfloat16 or wider, within the bound.
No kernel may reach another device: no remote copies, remote signals or barrier semaphores. Data moves between devices by JAX's collectives and lax.ppermute only.
A program may use at most 128 MiB of HBM per device.

```python
import math
import jax
import jax.numpy as jnp
import numpy as np
from jax import lax

D = 2048
FF = 1408
EXPERTS = 64
HEADS = 8
HD = 128
TOP = 4
TOK_DEV = 128
LENGTH = 512
SEQS = 64
CAP = 10
N_CTX = 4


def draw_query(key, part):
    key = jax.random.fold_in(key, 11)
    values = jax.random.normal(key, (SEQS, LENGTH, HEADS * HD), jnp.float32)
    return values.astype(jnp.bfloat16)


def draw_key_states(key, part):
    key = jax.random.fold_in(key, 23)
    values = jax.random.normal(key, (SEQS, LENGTH, HEADS * HD), jnp.float32)
    return values.astype(jnp.bfloat16)


def block_scale(stream_key, shape, shards, smallest, high):
    level, own = 1.0, jax.random.fold_in(stream_key, 6)
    for axis_at, shards_of in shards:
        heights = jnp.exp(jax.random.uniform(jax.random.fold_in(own, axis_at), (shards_of,), jnp.float32, smallest / len(shards), high / len(shards)))
        level = level * jnp.repeat(heights, shape[axis_at] // shards_of).reshape([-1 if axis == axis_at else 1 for axis in range(len(shape))])
    return level


def profile(count, total, limit, slope):
    portions = [(1 << 20) // math.isqrt(standing ** slope) + 1 for standing in range(2, count + 1)]
    spare, holding = total - limit - (count - 1), [1] * (count - 1)
    while spare > 0:
        free = [i for i in range(count - 1) if holding[i] < limit]
        whole, left = sum([portions[i] for i in free]), spare
        for i in free:
            extra = min(limit - holding[i], max(1, left * portions[i] // whole), spare)
            holding[i] = holding[i] + extra
            spare = spare - extra
    return np.array([limit] + holding)


def ragged(rng, count, total, bound, skew):
    if count == 2:
        one = jax.random.randint(rng, (), max(1, total - bound), min(bound, total - 1) + 1)
        return jnp.stack([one, total - one])
    lengths = jnp.asarray(profile(count, total, bound, skew), jnp.int32)
    twos = (count - 1) // 2
    giver, receiver = lengths[1:1 + 2 * twos:2], lengths[2:2 + 2 * twos:2]
    room = jnp.minimum(giver - 1, bound - receiver)
    passed = jax.random.randint(jax.random.fold_in(rng, 1), (twos,), 0, 1 << 20) % (room + 1)
    lengths = lengths.at[1:1 + 2 * twos:2].set(giver - passed).at[2:2 + 2 * twos:2].set(receiver + passed)
    return lengths[jax.random.permutation(jax.random.fold_in(rng, 2), count)]


def deal_out(key, own, number, rows, count, top, reach, lean):
    order = jax.random.permutation(key, count)
    heavy_load, common = portions_of(count, rows * top, reach, lean, True), portions_of(count, rows * top, reach, lean, False)
    places = jnp.arange(count)

    def named(sizes, offset_by):
        used = int((sizes > 0).sum())
        fixed = max(1, used // 4)
        moved = fixed + (places - fixed + offset_by * (used - fixed)) % max(1, count - fixed)
        return jnp.zeros((count,), jnp.int32).at[order[jnp.where(places < fixed, places, moved)]].set(jnp.asarray(sizes, jnp.int32))

    sizes = jnp.where(number % 4 == 0, named(heavy_load, number // 4), named(common, number - number // 4 - 1))
    mixed = jax.random.permutation(jax.random.fold_in(own, 3), count)
    source_of, taker = mixed[0:count // 2 * 2:2], mixed[1:count // 2 * 2:2]
    margin = jnp.minimum(sizes[source_of] - 1, reach - sizes[taker]) // 2
    margin = jnp.where((source_of == order[0]) | (taker == order[0]) | (sizes[taker] == 0), 0, jnp.maximum(margin, 0))
    moved = jax.random.randint(jax.random.fold_in(own, 4), (count // 2,), 0, 1 << 20) % (margin + 1)
    sizes = sizes.at[source_of].add(-moved).at[taker].add(moved)
    items = jnp.searchsorted(jnp.cumsum(sizes), jnp.arange(rows * top), side="right").astype(jnp.int32)
    listing = items.reshape(top, rows).T
    listing = listing[jax.random.permutation(jax.random.fold_in(own, 1), rows)]
    offset_by = jax.random.randint(jax.random.fold_in(own, 2), (rows, 1), 0, top)
    return jnp.take_along_axis(listing, (jnp.arange(top)[None, :] + offset_by) % top, axis=1)


def portions_of(number_of, total, reach, skew, full):
    loads = [(1 << 20) // math.isqrt(rank ** skew) + 1 for rank in range(1, number_of + 1)]
    largest = reach if full else min(reach, max(-(-total // number_of), total * loads[0] // sum(loads)))
    least = 1 if total - largest >= number_of - 1 else 0
    holding, rest = [largest] + [least] * (number_of - 1), total - largest - least * (number_of - 1)
    while rest > 0:
        candidates = [i for i in range(1, number_of) if holding[i] < largest] or [i for i in range(1, number_of) if holding[i] < reach]
        pool, budget = sum([loads[i] for i in candidates]), rest
        for i in candidates:
            extra = min(reach - holding[i], max(1, budget * loads[i] // pool), rest)
            holding[i] = holding[i] + extra
            rest = rest - extra
    return np.array(holding)


def centred(stream_key, dims, width, reach, cuts=(), held_as=jnp.bfloat16):
    entries = jax.random.normal(stream_key, dims, jnp.float32) * width
    if len(cuts) > 0:
        entries = block_scale(stream_key, dims, cuts, -0.22, 0.18) * entries
    return jnp.clip(entries, min=-reach, max=reach).astype(held_as)


def setup_inputs(seed: int = 0) -> dict:
    seeds = jax.random.split(jax.random.key(seed), 14)
    query = draw_query(jax.random.fold_in(seeds[13], 71), 0)
    key_states = draw_key_states(jax.random.fold_in(seeds[13], 71), 0)
    value_states = centred(seeds[2], (SEQS, LENGTH, HEADS * HD), 1.0, 6.0, ((0, 64), (1, 4)))
    segment_ids = jax.vmap(lambda own: jnp.searchsorted(jnp.cumsum(ragged(own, max(4, LENGTH // 64), LENGTH, LENGTH // 2, 1)), jnp.arange(LENGTH), side="right"))(jax.random.split(seeds[3], SEQS)).reshape((SEQS, LENGTH)).astype(jnp.int32)
    out_weight = centred(seeds[4], (HEADS * HD, D), (HEADS * HD) ** -0.5, 0.1875, ((0, 4),))
    grad_out = centred(seeds[5], (SEQS, LENGTH, D), 1.0, 6.0, ((0, 64), (1, 4)))
    routes_keys = jax.random.split(jax.random.fold_in(seeds[6], 1), SEQS * LENGTH // TOK_DEV)
    routes_turns = jax.random.permutation(jax.random.fold_in(seeds[6], 3), SEQS * LENGTH // TOK_DEV)
    routes = jax.vmap(lambda own, number: deal_out(jax.random.fold_in(seeds[6], 2), own, number, TOK_DEV, EXPERTS, TOP, CAP, 2))(routes_keys, routes_turns).reshape((SEQS, LENGTH, TOP))
    route_gates = jnp.clip(jnp.exp(math.log(0.6) - 2.4849067 * jax.random.uniform(seeds[7], (SEQS, LENGTH, TOP), jnp.float32) ** block_scale(seeds[7], (SEQS, LENGTH, TOP), ((0, 64), (1, 4)), -0.2, 0.2)), 0.05, 0.6)
    w_gate = centred(seeds[8], (EXPERTS, D, FF), D ** -0.5, 0.125, ((0, 64), (2, 4)))
    w_up = centred(seeds[9], (EXPERTS, D, FF), D ** -0.5, 0.125, ((0, 64), (2, 4)))
    w_down = centred(seeds[10], (EXPERTS, D, FF), FF ** -0.5, 0.15625, ((0, 64), (2, 4)))
    saved_gate = centred(seeds[11], (EXPERTS, N_CTX * SEQS * CAP, FF), 1.5, 8.0, ((0, 64), (1, 4)))
    saved_up = centred(seeds[12], (EXPERTS, N_CTX * SEQS * CAP, FF), 1.5, 8.0, ((0, 64), (1, 4)))
    return dict(query=query, key_states=key_states, value_states=value_states, segment_ids=segment_ids, out_weight=out_weight, grad_out=grad_out, routes=routes, route_gates=route_gates, w_gate=w_gate, w_up=w_up, w_down=w_down, saved_gate=saved_gate, saved_up=saved_up)


def slot_numbers(expert_ids, experts_all):
    table = (expert_ids[..., None] == jnp.arange(experts_all, dtype=jnp.int32)).astype(jnp.int32)
    earlier = jnp.cumsum(table, axis=-2) - table
    return lax.optimization_barrier(jnp.sum(earlier * table, axis=-1)).astype(jnp.int32)

def expert_backward(parts):
    routed_rows, gate_matrix, up_matrix, down_matrix, gate_saved, up_saved = parts
    hidden_grad = jnp.dot(routed_rows, down_matrix, preferred_element_type=jnp.float32)
    gate_pre = gate_saved.astype(jnp.float32)
    up_pre = up_saved.astype(jnp.float32)
    sigmoid_gate = jax.nn.sigmoid(gate_pre)
    grad_gate = (hidden_grad * up_pre * sigmoid_gate * (1.0 + gate_pre * (1.0 - sigmoid_gate))).astype(jnp.bfloat16)
    grad_up = (hidden_grad * gate_pre * sigmoid_gate).astype(jnp.bfloat16)
    summed = jnp.dot(grad_gate, gate_matrix.T, preferred_element_type=jnp.float32)
    summed = summed + jnp.dot(grad_up, up_matrix.T, preferred_element_type=jnp.float32)
    return summed.astype(jnp.bfloat16)

def attend(parts):
    query_rows, key_rows, value_rows, grad_rows, segments = parts
    scale = 1.0 / math.sqrt(HD)
    queries = query_rows.reshape(LENGTH, HEADS, HD).astype(jnp.float32)
    keys_all = key_rows.reshape(LENGTH, HEADS, HD).astype(jnp.float32)
    values_all = value_rows.reshape(LENGTH, HEADS, HD).astype(jnp.float32)
    grads = grad_rows.reshape(LENGTH, HEADS, HD).astype(jnp.float32)
    scores = jnp.einsum('ihd,jhd->hij', queries, keys_all) * scale
    position = jnp.arange(LENGTH, dtype=jnp.int32)
    causal = position[None, :] <= position[:, None]
    image = (segments[:, None] == segments[None, :]) & (segments % 2 == 1)[:, None]
    allowed = (causal | image)[None]
    scores = jnp.where(allowed, scores, -jnp.inf)
    row_max = lax.optimization_barrier(jnp.max(scores, axis=2, keepdims=True))
    expd = jnp.exp(scores - row_max)
    probs = expd / lax.optimization_barrier(jnp.sum(expd, axis=2, keepdims=True))
    probs_b = lax.optimization_barrier(probs.astype(jnp.bfloat16)).astype(jnp.float32)
    attn_out = jnp.einsum('hij,jhd->ihd', probs_b, values_all)
    delta = lax.optimization_barrier(jnp.sum(grads * attn_out, axis=2))
    dprobs = jnp.einsum('ihd,jhd->hij', grads, values_all)
    dscores = probs * (dprobs - delta.T[:, :, None])
    dscores = lax.optimization_barrier(dscores.astype(jnp.bfloat16)).astype(jnp.float32)
    grad_query = (jnp.einsum('hij,jhd->ihd', dscores, keys_all) * scale).astype(jnp.bfloat16)
    grad_key = (jnp.einsum('hij,ihd->jhd', dscores, queries) * scale).astype(jnp.bfloat16)
    grad_value = jnp.einsum('hij,ihd->jhd', probs_b, grads).astype(jnp.bfloat16)
    return (grad_query.reshape(LENGTH, HEADS * HD), grad_key.reshape(LENGTH, HEADS * HD), grad_value.reshape(LENGTH, HEADS * HD))

def reference(query, key_states, value_states, segment_ids, out_weight, grad_out, routes, route_gates, w_gate, w_up, w_down, saved_gate, saved_up):
    slots = slot_numbers(routes.reshape(SEQS * N_CTX, TOK_DEV * TOP), EXPERTS).reshape(SEQS, LENGTH, TOP)
    blocks = (jnp.arange(LENGTH, dtype=jnp.int32) // TOK_DEV)[None, :, None]
    sequence = jnp.arange(SEQS, dtype=jnp.int32)[:, None, None]
    row_index = (blocks * (SEQS * CAP) + sequence * CAP + slots).astype(jnp.int32)
    buffer_rows = N_CTX * SEQS * CAP

    def place(number, dispatched):
        scaled = (route_gates[number][:, :, None] * grad_out[number][:, None, :].astype(jnp.float32)).astype(jnp.bfloat16)
        return dispatched.at[routes[number], row_index[number]].set(scaled)
    dispatched = lax.fori_loop(0, SEQS, place, jnp.zeros((EXPERTS, buffer_rows, D), jnp.bfloat16))
    returned = lax.map(expert_backward, (dispatched, w_gate, w_up, w_down, saved_gate, saved_up))

    def combine(parts):
        grad_rows, expert_ids, row_ids = parts
        picked = returned[expert_ids, row_ids].astype(jnp.float32)
        return (grad_rows.astype(jnp.float32) + lax.optimization_barrier(jnp.sum(picked, axis=1))).astype(jnp.bfloat16)
    d_hidden = lax.map(combine, (grad_out, routes, row_index))
    grad_attn = jnp.dot(d_hidden.reshape(SEQS * LENGTH, D), out_weight.T, preferred_element_type=jnp.float32)
    grad_attn = grad_attn.astype(jnp.bfloat16).reshape(SEQS, LENGTH, HEADS * HD)
    grad_query, grad_key, grad_value = lax.map(attend, (query, key_states, value_states, grad_attn, segment_ids))
    return (d_hidden, grad_query, grad_key, grad_value)
```

```python
import functools
import math

import jax
import jax.numpy as jnp
from jax import lax
from jax.experimental import pallas as pl
from jax.experimental.pallas import tpu as pltpu
from jax.sharding import Mesh
from jax.sharding import PartitionSpec as P

D = 2048
HEADS = 8
HD = 128
EXPERTS = 64
CAP = 10
TOK = 128
RING = 8
RING_AXES = ("zh", "zl")
PLANE_AXES = ("x", "y")
PLANE = 16
HALF_ROWS = EXPERTS * CAP
CHUNKS = 2
F32 = jnp.float32
BF16 = jnp.bfloat16


def ring_shift(value, step):
    return lax.ppermute(value, RING_AXES, [(i, (i + step) % RING) for i in range(RING)])


def swap(value, axis):
    return lax.ppermute(value, axis, [(0, 1), (1, 0)])


def plane_exchange(rows):
    width = rows.shape[1]
    return lax.all_to_all(
        rows.reshape(PLANE, HALF_ROWS // PLANE, width), PLANE_AXES, 0, 0, tiled=True
    ).reshape(HALF_ROWS, width)


def together(*values):
    return lax.optimization_barrier(values)


def route_table(routes, route_gates):
    ids = routes[0]
    experts = jnp.arange(EXPERTS, dtype=jnp.int32)
    named = (ids[:, :, None] == experts).astype(F32)
    table = jnp.sum(named, axis=1)
    position = jnp.arange(TOK, dtype=jnp.int32)
    earlier = (position[None, :] < position[:, None]).astype(BF16)
    before = jnp.dot(earlier, table.astype(BF16), preferred_element_type=F32)
    slot = jnp.sum(named * before[:, None, :], axis=2)
    codes = ids.astype(F32) * 16.0 + slot
    return jnp.concatenate([codes.T, route_gates[0].T], axis=0)


NEAR = (-3, -2, -1, 0, 1, 2, 3)
FAR = (1, 2, 3, 4, -3, -2, -1)
SAVED_ROWS = (256, 256, 128)
MIB = 1024 * 1024


SCALARS = pl.BlockSpec(memory_space=pltpu.SMEM)


def saved_kernel(at_ref, gate_ref, up_ref, own_ref, *outs):
    units = gate_ref.shape[1] // 2
    step = pl.program_id(0)
    first = 0
    for high in range(2):

        @pl.when(at_ref[0] == high)
        def _():
            mine = slice(high * units, (high + 1) * units)
            own_ref[:, :units] = gate_ref[:, mine]
            own_ref[:, units:] = up_ref[:, mine]

    for ref, rows in zip(outs, SAVED_ROWS):
        for high in range(2):

            @pl.when((at_ref[0] == high) & (step >= first) & (step < first + rows // TOK))
            def _():
                other = slice((1 - high) * units, (2 - high) * units)
                ref[:, :units] = gate_ref[:, other]
                ref[:, units:] = up_ref[:, other]

        first += rows // TOK


def split_saved(at, saved_gate, saved_up):
    width = saved_gate.shape[1]
    by_rows = pl.BlockSpec((TOK, width), lambda i: (i, 0))
    parts, shapes, first = [], [], 0
    for rows in SAVED_ROWS:
        count = rows // TOK
        parts.append(
            pl.BlockSpec(
                (TOK, width),
                lambda i, first=first, count=count: (jnp.clip(i - first, 0, count - 1), 0),
            )
        )
        shapes.append(jax.ShapeDtypeStruct((rows, width), BF16))
        first += count
    own, *other = pl.pallas_call(
        saved_kernel,
        grid=(HALF_ROWS // TOK,),
        in_specs=[SCALARS, by_rows, by_rows],
        out_specs=[by_rows, *parts],
        out_shape=[jax.ShapeDtypeStruct(saved_gate.shape, BF16), *shapes],
        compiler_params=pltpu.CompilerParams(vmem_limit_bytes=24 * MIB),
    )(at, saved_gate, saved_up)
    return own, other


def dispatch_kernel(at_ref, *refs):
    tables, blocks = refs[0], refs[1:8]
    rows_ref, select_ref, tokens, row_gate = refs[8:]
    z_low = at_ref[1]

    for low in range(4):

        @pl.when(z_low == low)
        def _():
            for source in range(4):
                tokens[source * TOK : (source + 1) * TOK, :] = blocks[source + 3 - low][...]

        @pl.when((z_low == low) & (pl.program_id(0) == 0))
        def _():
            total = jnp.zeros((HALF_ROWS, 1), F32)
            numbers = lax.broadcasted_iota(jnp.int32, (HALF_ROWS, TOK), 0)
            for source in range(4):
                table = tables[source]
                codes = table[:4].astype(jnp.int32)
                expert = codes >> 4
                row = (expert >> 2) * (4 * CAP) + source * CAP + (codes & 15)
                row = jnp.where((expert & 3) == low, row, -1)
                marks = jnp.zeros((HALF_ROWS, TOK), F32)
                gates = jnp.zeros((HALF_ROWS, TOK), F32)
                for choice in range(4):
                    hit = numbers == row[choice : choice + 1]
                    marks = jnp.where(hit, 1.0, marks)
                    gates = jnp.where(hit, table[4 + choice : 5 + choice], gates)
                select_ref[:, source * TOK : (source + 1) * TOK] = marks.astype(BF16)
                total = total + jnp.sum(gates, axis=1, keepdims=True)
            row_gate[...] = total

    picked = jnp.dot(select_ref[...], tokens[...], preferred_element_type=F32)
    rows_ref[...] = (picked * row_gate[...]).astype(BF16)


def dispatch(at, tables, half, blocks):
    width = 512
    return pl.pallas_call(
        dispatch_kernel,
        grid=(D // width,),
        in_specs=[SCALARS]
        + [pl.BlockSpec((4, 8, TOK), lambda j: (0, 0, 0))]
        + [pl.BlockSpec((TOK, width), lambda j: (0, j))] * 7,
        out_specs=[
            pl.BlockSpec((HALF_ROWS, width), lambda j: (0, j)),
            pl.BlockSpec((HALF_ROWS, 4 * TOK), lambda j: (0, 0)),
        ],
        out_shape=[
            jax.ShapeDtypeStruct((HALF_ROWS, D), BF16),
            jax.ShapeDtypeStruct((HALF_ROWS, 4 * TOK), BF16),
        ],
        scratch_shapes=[pltpu.VMEM((4 * TOK, width), BF16), pltpu.VMEM((HALF_ROWS, 1), F32)],
        compiler_params=pltpu.CompilerParams(vmem_limit_bytes=40 * MIB),
    )(at, lax.dynamic_slice_in_dim(tables, 4 * half, 4, axis=0), *blocks)


def expert_kernel(at_ref, rows_ref, *refs, parts):
    saved, weights, refs = refs[:parts], refs[parts : parts + 6], refs[parts + 6 :]
    *outs, down, gate, up, grad_gate, grad_up, sems = refs
    piece = weights[0].shape[0]
    units = 2 * piece
    step = pl.program_id(0)
    width = outs[0].shape[1]

    @pl.when(step == 0)
    def _():
        copies = []
        for number, ref in enumerate(weights):
            where = at_ref[2] if number % 2 == 0 else 1 - at_ref[2]
            start = pl.multiple_of(where * piece, 16)
            target = (down, gate, up)[number // 2].at[pl.ds(start, piece), :]
            copies.append(pltpu.make_async_copy(ref, target, sems.at[number]))
        for copy in copies:
            copy.start()
        for copy in copies[:2]:
            copy.wait()
        first = 0
        for ref in saved:
            rows = slice(first, first + ref.shape[0])
            first += ref.shape[0]
            hidden_grad = lax.dot_general(
                rows_ref[rows, :],
                down[...],
                (((1,), (1,)), ((), ())),
                preferred_element_type=F32,
            )
            gate_pre = ref[:, :units].astype(F32)
            up_pre = ref[:, units:].astype(F32)
            sigmoid_gate = jax.nn.sigmoid(gate_pre)
            grad_gate[rows, :] = (
                hidden_grad * up_pre * sigmoid_gate * (1.0 + gate_pre * (1.0 - sigmoid_gate))
            ).astype(BF16)
            grad_up[rows, :] = (hidden_grad * gate_pre * sigmoid_gate).astype(BF16)
        for copy in copies[2:]:
            copy.wait()

    columns = pl.ds(pl.multiple_of(step * width, 128), width)
    total = jnp.dot(grad_gate[...], gate[:, columns], preferred_element_type=F32)
    total = total + jnp.dot(grad_up[...], up[:, columns], preferred_element_type=F32)
    total = total.astype(BF16)
    each = pl.num_programs(0) // len(outs)
    for number, out in enumerate(outs):

        @pl.when((step >= number * each) & (step < (number + 1) * each))
        def _():
            out[...] = total


def expert_back(at, rows, saved, weights, chunks):
    steps, each = 4, 4 // chunks
    width = D // steps
    units = saved[0].shape[1] // 2
    constant = lambda value: pl.BlockSpec(value.shape, lambda j: (0, 0))
    return pl.pallas_call(
        functools.partial(expert_kernel, parts=len(saved)),
        grid=(steps,),
        in_specs=[SCALARS, constant(rows)]
        + [constant(part) for part in saved]
        + [pl.BlockSpec(memory_space=pl.ANY)] * len(weights),
        out_specs=[
            pl.BlockSpec(
                (HALF_ROWS, width),
                lambda j, number=number: (0, jnp.clip(j - number * each, 0, each - 1)),
            )
            for number in range(chunks)
        ],
        out_shape=[jax.ShapeDtypeStruct((HALF_ROWS, D // chunks), BF16)] * chunks,
        scratch_shapes=[pltpu.VMEM((units, D), BF16)] * 3
        + [pltpu.VMEM((HALF_ROWS, units), BF16)] * 2
        + [pltpu.SemaphoreType.DMA((len(weights),))],
        compiler_params=pltpu.CompilerParams(vmem_limit_bytes=48 * MIB),
    )(at, rows, *saved, *weights)


def combine(select, returned):
    return lax.dot_general(
        select, returned, (((0,), (0,)), ((), ())), preferred_element_type=F32
    )


class RingSum:
    def __init__(self, own, other, z_high, z_low):
        self.width = own.shape[1]
        self.own, self.other = own, other
        self.z_high, self.z_low = z_high, z_low

    def at(self, step):
        target = (self.z_high * 4 + self.z_low + step + RING) % RING
        start = (target % 4) * TOK
        own, other = (
            lax.dynamic_slice_in_dim(terms, start, TOK, axis=0) for terms in (self.own, self.other)
        )
        return jnp.where(target // 4 == self.z_high, own, other)

    def first(self):
        half = self.width // 2
        far = self.at(4)
        self.up = ring_shift(far[:, :half].astype(BF16), 1)
        self.down = ring_shift(far[:, half:].astype(BF16), -1)

    def next(self, step):
        half = self.width // 2
        ahead, behind = self.at(step), self.at(-step)
        up, down = self.up.astype(F32), self.down.astype(F32)
        if step == 3:
            ahead = jnp.concatenate([ahead[:, :half] + up, ahead[:, half:]], axis=1)
            behind = jnp.concatenate([behind[:, :half], behind[:, half:] + down], axis=1)
        else:
            ahead, behind = ahead + up, behind + down
        self.up = ring_shift(ahead.astype(BF16), 1)
        self.down = ring_shift(behind.astype(BF16), -1)

    def total(self):
        return self.at(0) + self.up.astype(F32) + self.down.astype(F32)


def own_features(value, core):
    a, b, c, d = (value[..., 256 * i : 256 * (i + 1)] for i in range(4))
    first = core == 0
    mine = jnp.concatenate([jnp.where(first, a, b), jnp.where(first, c, d)], axis=-1)
    theirs = jnp.concatenate([jnp.where(first, b, a), jnp.where(first, d, c)], axis=-1)
    return mine, theirs


def all_features(mine, theirs, core):
    first = core == 0
    low, high = slice(0, 256), slice(256, 512)
    return jnp.concatenate(
        [
            jnp.where(first, mine[:, low], theirs[:, low]),
            jnp.where(first, theirs[:, low], mine[:, low]),
            jnp.where(first, mine[:, high], theirs[:, high]),
            jnp.where(first, theirs[:, high], mine[:, high]),
        ],
        axis=1,
    )


def attention_kernel(q_ref, k_ref, v_ref, g_ref, mask_ref, dq_ref, dk_ref, dv_ref, far_ref):
    scale = 1.0 / math.sqrt(HD)
    here = q_ref.shape[0]
    queries, keys, values, grads = q_ref[...], k_ref[...], v_ref[...], g_ref[...]
    last = (((1,), (1,)), ((), ()))
    rows = (((0,), (0,)), ((), ()))
    scores = lax.dot_general(queries, keys, last, preferred_element_type=F32) * scale
    scores = jnp.where(mask_ref[...] > 0.0, scores, -jnp.inf)
    expd = jnp.exp(scores - jnp.max(scores, axis=1, keepdims=True))
    probs = expd / jnp.sum(expd, axis=1, keepdims=True)
    probs_b = probs.astype(BF16)
    attn_out = jnp.dot(probs_b, values, preferred_element_type=F32)
    delta = jnp.sum(grads.astype(F32) * attn_out, axis=1, keepdims=True)
    dprobs = lax.dot_general(grads, values, last, preferred_element_type=F32)
    dscores = (probs * (dprobs - delta)).astype(BF16)
    dq_ref[...] = (jnp.dot(dscores, keys, preferred_element_type=F32) * scale).astype(BF16)
    grad_key = lax.dot_general(dscores, queries, rows, preferred_element_type=F32) * scale
    grad_value = lax.dot_general(probs_b, grads, rows, preferred_element_type=F32)
    dk_ref[...] = grad_key[:here]
    dv_ref[...] = grad_value[:here]
    far_ref[0] = grad_key[here:].astype(BF16)
    far_ref[1] = grad_value[here:].astype(BF16)


def attention_backward(queries, keys, values, grads, mask):
    here, features = queries.shape
    everywhere = keys.shape[0]
    heads = features // HD
    by_head = lambda rows: pl.BlockSpec((rows, HD), lambda h: (0, h))
    return pl.pallas_call(
        attention_kernel,
        grid=(heads,),
        in_specs=[
            by_head(here),
            by_head(everywhere),
            by_head(everywhere),
            by_head(here),
            pl.BlockSpec((here, everywhere), lambda h: (0, 0)),
        ],
        out_specs=[
            by_head(here),
            by_head(here),
            by_head(here),
            pl.BlockSpec((2, here, HD), lambda h: (0, 0, h)),
        ],
        out_shape=[
            jax.ShapeDtypeStruct((here, features), BF16),
            jax.ShapeDtypeStruct((here, features), F32),
            jax.ShapeDtypeStruct((here, features), F32),
            jax.ShapeDtypeStruct((2, here, features), BF16),
        ],
        compiler_params=pltpu.CompilerParams(vmem_limit_bytes=32 * 1024 * 1024),
    )(queries, keys, values, grads, mask)


def on_device(
    query,
    key_states,
    value_states,
    segment_ids,
    out_weight,
    grad_out,
    routes,
    route_gates,
    w_gate,
    w_up,
    w_down,
    saved_gate,
    saved_up,
):
    z_high, core, z_low = lax.axis_index("zh"), lax.axis_index("core"), lax.axis_index("zl")
    plane = lax.axis_index(PLANE_AXES)
    tokens = grad_out[0]

    at = jnp.stack([z_high, z_low, core]).astype(jnp.int32)

    half = TOK // 2
    blocks = {0: tokens}
    blocks[1], blocks[-1] = ring_shift(tokens, -1), ring_shift(tokens, 1)
    table = route_table(routes, route_gates)
    saved_own, saved_leaving = split_saved(at, saved_gate[0], saved_up[0])
    blocks[1], blocks[-1], table = together(blocks[1], blocks[-1], table)

    blocks[2], blocks[-2] = ring_shift(blocks[1], -1), ring_shift(blocks[-1], 1)
    tables = lax.all_to_all(
        jnp.broadcast_to(table[None], (RING, 8, TOK)), RING_AXES, 0, 0, tiled=True
    )
    strip = out_weight.shape[0] // PLANE
    own_strip, _ = together(
        lax.dynamic_slice_in_dim(out_weight, plane * strip, strip, axis=0), table
    )
    fetched = swap(own_strip, "zh")
    blocks[2], blocks[-2], fetched, tables, saved_leaving = together(
        blocks[2], blocks[-2], fetched, tables, saved_leaving
    )

    blocks[3], blocks[-3] = ring_shift(blocks[2], -1), ring_shift(blocks[-2], 1)
    weight_far = lax.all_to_all(
        jnp.broadcast_to(fetched[None], (PLANE, strip, D)), PLANE_AXES, 0, 0, tiled=True
    ).reshape(out_weight.shape)
    blocks[3], blocks[-3], weight_far = together(blocks[3], blocks[-3], weight_far)

    last_up, last_down = ring_shift(blocks[3][:half], -1), ring_shift(blocks[-3][half:], 1)
    leaving_rows, select_own = dispatch(at, tables, z_high, [blocks[i] for i in NEAR])
    rows_own = plane_exchange(leaving_rows)
    last_up, last_down, saved_leaving = together(last_up, last_down, saved_leaving)
    blocks[4] = jnp.concatenate([last_up, last_down], axis=0)
    saved_other = [swap(saved_leaving[0], "zh")]
    leaving_rows, select_other = dispatch(at, tables, 1 - z_high, [blocks[i] for i in FAR])
    weights = []
    for weight in (w_down, w_gate, w_up):
        piece = jnp.swapaxes(weight[0], 0, 1)
        weights += [piece, swap(piece, "core")]

    heads_mine, heads_theirs = [], []
    for value in (query[0], key_states[0], value_states[0]):
        mine, theirs = own_features(value, core)
        heads_mine.append(mine)
        heads_theirs.append(theirs)
    heads_theirs = jnp.concatenate(heads_theirs, axis=1)
    heads_theirs, segment_mine, _ = together(heads_theirs, segment_ids, last_up)
    heads_chip = jnp.concatenate(
        [jnp.concatenate(heads_mine, axis=1), swap(heads_theirs, "core")], axis=0
    )
    segment_chip = jnp.concatenate([segment_mine, swap(segment_mine, "core")], axis=1)
    segment_keys = jnp.concatenate([segment_chip, swap(segment_chip, "zh")], axis=1)[0]
    rows_own, leaving_rows, saved_own, heads_chip, segment_keys, saved_other[0], saved_next = together(
        rows_own, leaving_rows, saved_own, heads_chip, segment_keys, saved_other[0], saved_leaving[1]
    )

    rows_other = plane_exchange(leaving_rows)
    saved_other.append(swap(saved_next, "zh"))
    (leaving_own,) = expert_back(at, rows_own, [saved_own], weights, 1)
    offsets = jnp.arange(TOK, dtype=jnp.int32)
    place = lambda high, which: (high * 2 + which) * TOK + offsets
    chip_place = jnp.concatenate([place(z_high, core), place(z_high, 1 - core)])
    key_place = jnp.concatenate([chip_place, place(1 - z_high, core), place(1 - z_high, 1 - core)])
    segment_here = segment_keys[: 2 * TOK, None]
    causal = key_place[None, :] <= chip_place[:, None]
    image = (segment_here == segment_keys[None, :]) & (segment_here % 2 == 1)
    mask = (causal | image).astype(F32)
    projection = jnp.where(
        z_high == 0,
        jnp.concatenate([out_weight, weight_far], axis=0),
        jnp.concatenate([weight_far, out_weight], axis=0),
    )
    rows_other, leaving_own, mask, projection, saved_other[1], saved_next = together(
        rows_other, leaving_own, mask, projection, saved_other[1], saved_leaving[2]
    )

    back_own = plane_exchange(leaving_own)
    saved_other.append(swap(saved_next, "zh"))
    queries, key_value, saved_other[2] = together(
        heads_chip[:, :512], heads_chip[:, 512:], saved_other[2]
    )
    key_value_far = swap(key_value, "zh")
    leaving = expert_back(at, rows_other, saved_other, weights, CHUNKS)
    width = D // CHUNKS
    columns = [slice(i * width, (i + 1) * width) for i in range(CHUNKS)]
    back_own, leaving = together(back_own, leaving)
    returning = plane_exchange(leaving[0])
    terms_own = combine(select_own, back_own)
    returning, second_leaving, terms_own, key_value_far = together(
        returning, leaving[1], terms_own, key_value_far
    )

    sums = [None, None]
    returning_next = plane_exchange(second_leaving)
    sums[0] = RingSum(terms_own[:, columns[0]], combine(select_other, returning), z_high, z_low)
    sums[0].first()
    sums[0].up, sums[0].down = together(sums[0].up, sums[0].down)
    sums[0].next(3)
    sums[0].up, sums[0].down, returning_next = together(sums[0].up, sums[0].down, returning_next)
    sums[1] = RingSum(
        terms_own[:, columns[1]], combine(select_other, returning_next), z_high, z_low
    )
    sums[0].next(2)
    sums[1].first()

    def meet():
        sums[0].up, sums[0].down, sums[1].up, sums[1].down = together(
            sums[0].up, sums[0].down, sums[1].up, sums[1].down
        )

    meet()
    sums[0].next(1)
    sums[1].next(3)
    meet()
    hidden = []

    def finish(part):
        piece = (tokens[:, columns[part]].astype(F32) + sums[part].total()).astype(BF16)
        hidden.append(piece)
        chip_hidden = jnp.concatenate([piece, swap(piece, "core")], axis=0)
        return lax.dot_general(
            chip_hidden,
            projection[:, columns[part]],
            (((1,), (1,)), ((), ())),
            preferred_element_type=F32,
        )

    sums[1].next(2)
    grad_attn = finish(0)
    sums[1].up, sums[1].down, grad_attn = together(sums[1].up, sums[1].down, grad_attn)
    sums[1].next(1)
    grad_attn = (grad_attn + finish(1)).astype(BF16)
    d_hidden = jnp.concatenate(hidden, axis=1)

    keys = jnp.concatenate([key_value[:, :512], key_value_far[:, :512]], axis=0)
    values = jnp.concatenate([key_value[:, 512:], key_value_far[:, 512:]], axis=0)
    grad_query, grad_key, grad_value, leaving = attention_backward(
        queries, keys, values, grad_attn, mask
    )
    arrived = swap(leaving, "zh").astype(F32)
    outs = []
    for grad in (
        grad_query,
        (grad_key + arrived[0]).astype(BF16),
        (grad_value + arrived[1]).astype(BF16),
    ):
        outs.append(all_features(grad[:TOK], swap(grad[TOK:], "core"), core)[None])
    return (d_hidden[None], *outs)


def solution(mesh):
    fine = Mesh(mesh.devices.reshape(2, 2, 4, 4, 4), ("zh", "core", "x", "y", "zl"))
    exp = ("x", "y", "zl")
    ctx = ("zh", "core")
    in_specs = (
        P(exp, ctx, None),
        P(exp, ctx, None),
        P(exp, ctx, None),
        P(exp, ctx),
        P(ctx, None),
        P(exp, ctx, None),
        P(exp, ctx, None),
        P(exp, ctx, None),
        P(exp, None, ctx),
        P(exp, None, ctx),
        P(exp, None, ctx),
        P(exp, ctx, None),
        P(exp, ctx, None),
    )
    out_specs = (P(exp, ctx, None),) * 4
    return jax.shard_map(
        on_device, mesh=fine, in_specs=in_specs, out_specs=out_specs, check_vma=False
    )
```

```python
import functools
import math

import jax
import jax.numpy as jnp
from jax import lax
from jax.experimental import pallas as pl
from jax.experimental.pallas import tpu as pltpu
from jax.sharding import Mesh
from jax.sharding import PartitionSpec as P

D = 2048
HEADS = 8
HD = 128
EXPERTS = 64
CAP = 10
TOK = 128
RING = 8
RING_AXES = ("zh", "zl")
PLANE_AXES = ("x", "y")
PLANE = 16
HALF_ROWS = EXPERTS * CAP
F32 = jnp.float32
BF16 = jnp.bfloat16


def ring_shift(value, step):
    return lax.ppermute(value, RING_AXES, [(i, (i + step) % RING) for i in range(RING)])


def swap(value, axis):
    return lax.ppermute(value, axis, [(0, 1), (1, 0)])


def plane_exchange(rows):
    width = rows.shape[1]
    return lax.all_to_all(
        rows.reshape(PLANE, HALF_ROWS // PLANE, width), PLANE_AXES, 0, 0, tiled=True
    ).reshape(HALF_ROWS, width)


def together(*values):
    return lax.optimization_barrier(values)


def route_table(routes, route_gates, segments):
    ids = routes[0]
    experts = jnp.arange(EXPERTS, dtype=jnp.int32)
    named = (ids[:, :, None] == experts).astype(F32)
    table = jnp.sum(named, axis=1)
    position = jnp.arange(TOK, dtype=jnp.int32)
    earlier = (position[None, :] < position[:, None]).astype(BF16)
    before = jnp.dot(earlier, table.astype(BF16), preferred_element_type=F32)
    slot = jnp.sum(named * before[:, None, :], axis=2)
    codes = ids.astype(F32) * 16.0 + slot
    spare = jnp.zeros((6, TOK), F32)
    return jnp.concatenate([codes.T, route_gates[0].T, segments.astype(F32), spare], axis=0)


NEAR = (-3, -2, -1, 0, 1, 2, 3)
FAR = (1, 2, 3, 4, -3, -2, -1)
SAVED_ROWS = (256, 256, 128)
SAVED_BLOCK = 128
MIB = 1024 * 1024


SCALARS = pl.BlockSpec(memory_space=pltpu.SMEM)


def saved_kernel(at_ref, gate_ref, up_ref, own_ref, *outs):
    units = gate_ref.shape[1] // 2
    step = pl.program_id(0)
    first = 0
    for high in range(2):

        @pl.when(at_ref[0] == high)
        def _():
            mine = slice(high * units, (high + 1) * units)
            own_ref[:, :units] = gate_ref[:, mine]
            own_ref[:, units:] = up_ref[:, mine]

    for ref, rows in zip(outs, SAVED_ROWS):
        for high in range(2):

            @pl.when((at_ref[0] == high) & (step >= first) & (step < first + rows // SAVED_BLOCK))
            def _():
                other = slice((1 - high) * units, (2 - high) * units)
                ref[:, :units] = gate_ref[:, other]
                ref[:, units:] = up_ref[:, other]

        first += rows // SAVED_BLOCK


def split_saved(at, saved_gate, saved_up):
    width = saved_gate.shape[1]
    by_rows = pl.BlockSpec((SAVED_BLOCK, width), lambda i: (i, 0))
    parts, shapes, first = [], [], 0
    for rows in SAVED_ROWS:
        count = rows // SAVED_BLOCK
        parts.append(
            pl.BlockSpec(
                (SAVED_BLOCK, width),
                lambda i, first=first, count=count: (jnp.clip(i - first, 0, count - 1), 0),
            )
        )
        shapes.append(jax.ShapeDtypeStruct((rows, width), BF16))
        first += count
    own, *other = pl.pallas_call(
        saved_kernel,
        grid=(HALF_ROWS // SAVED_BLOCK,),
        in_specs=[SCALARS, by_rows, by_rows],
        out_specs=[by_rows, *parts],
        out_shape=[jax.ShapeDtypeStruct(saved_gate.shape, BF16), *shapes],
        compiler_params=pltpu.CompilerParams(vmem_limit_bytes=24 * MIB),
    )(at, saved_gate, saved_up)
    return own, other


def dispatch_kernel(at_ref, *refs):
    tables, blocks = refs[0], refs[1:8]
    rows_ref, collect_ref, select, tokens, row_gate = refs[8:]
    z_low = at_ref[1]

    for low in range(4):

        @pl.when(z_low == low)
        def _():
            for source in range(4):
                tokens[source * TOK : (source + 1) * TOK, :] = blocks[source + 3 - low][...]

        @pl.when((z_low == low) & (pl.program_id(0) == 0))
        def _():
            total = jnp.zeros((HALF_ROWS, 1), F32)
            numbers = lax.broadcasted_iota(jnp.int32, (HALF_ROWS, TOK), 0)
            for source in range(4):
                table = tables[source]
                codes = table[:4].astype(jnp.int32)
                expert = codes >> 4
                row = (expert >> 2) * (4 * CAP) + source * CAP + (codes & 15)
                row = jnp.where((expert & 3) == low, row, -1)
                marks = jnp.zeros((HALF_ROWS, TOK), F32)
                gates = jnp.zeros((HALF_ROWS, TOK), F32)
                for choice in range(4):
                    hit = numbers == row[choice : choice + 1]
                    marks = jnp.where(hit, 1.0, marks)
                    gates = jnp.where(hit, table[4 + choice : 5 + choice], gates)
                columns = slice(source * TOK, (source + 1) * TOK)
                select[:, columns] = marks.astype(BF16)
                collect_ref[columns, :] = marks.T.astype(BF16)
                total = total + jnp.sum(gates, axis=1, keepdims=True)
            row_gate[...] = total

    picked = jnp.dot(select[...], tokens[...], preferred_element_type=F32)
    rows_ref[...] = (picked * row_gate[...]).astype(BF16)


def dispatch(at, tables, half, blocks):
    width = 512
    return pl.pallas_call(
        dispatch_kernel,
        grid=(D // width,),
        in_specs=[SCALARS]
        + [pl.BlockSpec((4, 16, TOK), lambda j: (0, 0, 0))]
        + [pl.BlockSpec((TOK, width), lambda j: (0, j))] * 7,
        out_specs=[
            pl.BlockSpec((HALF_ROWS, width), lambda j: (0, j)),
            pl.BlockSpec((4 * TOK, HALF_ROWS), lambda j: (0, 0)),
        ],
        out_shape=[
            pltpu.HBM((HALF_ROWS, D), BF16),
            jax.ShapeDtypeStruct((4 * TOK, HALF_ROWS), BF16),
        ],
        scratch_shapes=[
            pltpu.VMEM((HALF_ROWS, 4 * TOK), BF16),
            pltpu.VMEM((4 * TOK, width), BF16),
            pltpu.VMEM((HALF_ROWS, 1), F32),
        ],
        compiler_params=pltpu.CompilerParams(vmem_limit_bytes=40 * MIB),
    )(at, lax.dynamic_slice_in_dim(tables, 4 * half, 4, axis=0), *blocks)


def expert_kernel(at_ref, *refs, parts):
    rows_hbm, saved_hbm = refs[0], refs[1 : 1 + parts]
    weights, refs = refs[1 + parts : 7 + parts], refs[7 + parts :]
    out_ref, rows_ref, saved, down, gate, up, grad_gate, grad_up, sems = refs
    piece = weights[0].shape[0]
    units = 2 * piece
    step = pl.program_id(0)
    width = out_ref.shape[1]

    @pl.when(step == 0)
    def _():
        copies = []
        for number, ref in enumerate(weights):
            where = at_ref[2] if number % 2 == 0 else 1 - at_ref[2]
            start = pl.multiple_of(where * piece, 16)
            target = (down, gate, up)[number // 2].at[pl.ds(start, piece), :]
            copies.append(pltpu.make_async_copy(ref, target, sems.at[number]))
        needed = [pltpu.make_async_copy(rows_hbm, rows_ref, sems.at[6])]
        first = 0
        for number, ref in enumerate(saved_hbm):
            target = saved.at[pl.ds(first, ref.shape[0]), :]
            needed.append(pltpu.make_async_copy(ref, target, sems.at[7 + number]))
            first += ref.shape[0]
        for copy in (*copies[:2], *needed, *copies[2:]):
            copy.start()
        for copy in (*copies[:2], *needed):
            copy.wait()
        for first in range(0, HALF_ROWS, 320):
            rows = slice(first, first + 320)
            hidden_grad = lax.dot_general(
                rows_ref[rows, :],
                down[...],
                (((1,), (1,)), ((), ())),
                preferred_element_type=F32,
            )
            gate_pre = saved[rows, :units].astype(F32)
            up_pre = saved[rows, units:].astype(F32)
            sigmoid_gate = jax.nn.sigmoid(gate_pre)
            grad_gate[rows, :] = (
                hidden_grad * up_pre * sigmoid_gate * (1.0 + gate_pre * (1.0 - sigmoid_gate))
            ).astype(BF16)
            grad_up[rows, :] = (hidden_grad * gate_pre * sigmoid_gate).astype(BF16)
        for copy in copies[2:]:
            copy.wait()

    columns = pl.ds(pl.multiple_of(step * width, 128), width)
    total = jnp.dot(grad_gate[...], gate[:, columns], preferred_element_type=F32)
    total = total + jnp.dot(grad_up[...], up[:, columns], preferred_element_type=F32)
    out_ref[...] = total.astype(BF16)


def expert_back(at, rows, saved, weights):
    width = 512
    units = saved[0].shape[1] // 2
    return pl.pallas_call(
        functools.partial(expert_kernel, parts=len(saved)),
        grid=(D // width,),
        in_specs=[SCALARS]
        + [pl.BlockSpec(memory_space=pl.ANY)] * (1 + len(saved) + len(weights)),
        out_specs=pl.BlockSpec((HALF_ROWS, width), lambda j: (0, j)),
        out_shape=pltpu.HBM((HALF_ROWS, D), BF16),
        scratch_shapes=[pltpu.VMEM((HALF_ROWS, D), BF16), pltpu.VMEM((HALF_ROWS, 2 * units), BF16)]
        + [pltpu.VMEM((units, D), BF16)] * 3
        + [pltpu.VMEM((HALF_ROWS, units), BF16)] * 2
        + [pltpu.SemaphoreType.DMA((7 + len(saved),))],
        compiler_params=pltpu.CompilerParams(vmem_limit_bytes=48 * MIB),
    )(at, rows, *saved, *weights)


def combine(collect, returned):
    return jnp.dot(collect, returned, preferred_element_type=F32).astype(BF16)


RING_STEPS = (4, 3, -3, 2, -2, 1, -1, 0)


def terms_kernel(at_ref, collect_ref, back_ref, own_ref, *refs):
    outs, other_ref = refs[:-1], refs[-1]
    other_ref[...] = combine(collect_ref[...], back_ref[...])
    for step, out in zip(RING_STEPS, outs):
        target = (at_ref[0] * 4 + at_ref[1] + step + RING) % RING
        rows = pl.ds(pl.multiple_of((target % 4) * TOK, TOK), TOK)
        out[...] = jnp.where(target // 4 == at_ref[0], own_ref[rows, :], other_ref[rows, :])


def ring_terms(at, collect_other, back_other, terms_own):
    width = 512
    rows, slots = collect_other.shape
    by_columns = lambda height: pl.BlockSpec((height, width), lambda j: (0, j))
    outs = pl.pallas_call(
        terms_kernel,
        grid=(D // width,),
        in_specs=[
            SCALARS,
            pl.BlockSpec((rows, slots), lambda j: (0, 0)),
            by_columns(slots),
            by_columns(rows),
        ],
        out_specs=[by_columns(TOK)] * len(RING_STEPS),
        out_shape=[jax.ShapeDtypeStruct((TOK, D), BF16)] * len(RING_STEPS),
        scratch_shapes=[pltpu.VMEM((rows, width), BF16)],
        compiler_params=pltpu.CompilerParams(vmem_limit_bytes=40 * MIB),
    )(at, collect_other, back_other, terms_own)
    return dict(zip(RING_STEPS, outs))


def own_features(value, core):
    a, b, c, d = (value[..., 256 * i : 256 * (i + 1)] for i in range(4))
    first = core == 0
    mine = jnp.concatenate([jnp.where(first, a, b), jnp.where(first, c, d)], axis=-1)
    theirs = jnp.concatenate([jnp.where(first, b, a), jnp.where(first, d, c)], axis=-1)
    return mine, theirs


def all_features(mine, theirs, core):
    first = core == 0
    low, high = slice(0, 256), slice(256, 512)
    return jnp.concatenate(
        [
            jnp.where(first, mine[:, low], theirs[:, low]),
            jnp.where(first, theirs[:, low], mine[:, low]),
            jnp.where(first, mine[:, high], theirs[:, high]),
            jnp.where(first, theirs[:, high], mine[:, high]),
        ],
        axis=1,
    )


def attention_kernel(
    at_ref,
    q_ref,
    k_ref,
    v_ref,
    near_hidden_ref,
    far_hidden_ref,
    near_weight_ref,
    far_weight_ref,
    mask_ref,
    dq_ref,
    dk_ref,
    dv_ref,
    far_ref,
    grads_ref,
):
    scale = 1.0 / math.sqrt(HD)
    here = q_ref.shape[0]
    head = pl.program_id(0)
    queries, keys, values = q_ref[...], k_ref[...], v_ref[...]
    last = (((1,), (1,)), ((), ()))
    rows_here = pl.ds(pl.multiple_of((head % 2) * HD, HD), HD)
    weight = jnp.where(
        head // 2 == at_ref[0], near_weight_ref[rows_here, :], far_weight_ref[rows_here, :]
    )
    for number, ref in enumerate((near_hidden_ref, far_hidden_ref)):
        grads_ref[number * TOK : (number + 1) * TOK, :] = lax.dot_general(
            ref[...], weight, last, preferred_element_type=F32
        ).astype(BF16)
    grads = grads_ref[...]
    rows = (((0,), (0,)), ((), ()))
    scores = lax.dot_general(queries, keys, last, preferred_element_type=F32) * scale
    scores = jnp.where(mask_ref[...] > 0.0, scores, -jnp.inf)
    expd = jnp.exp(scores - jnp.max(scores, axis=1, keepdims=True))
    probs = expd / jnp.sum(expd, axis=1, keepdims=True)
    probs_b = probs.astype(BF16)
    attn_out = jnp.dot(probs_b, values, preferred_element_type=F32)
    delta = jnp.sum(grads.astype(F32) * attn_out, axis=1, keepdims=True)
    dprobs = lax.dot_general(grads, values, last, preferred_element_type=F32)
    dscores = (probs * (dprobs - delta)).astype(BF16)
    dq_ref[...] = (jnp.dot(dscores, keys, preferred_element_type=F32) * scale).astype(BF16)
    grad_key = lax.dot_general(dscores, queries, rows, preferred_element_type=F32) * scale
    grad_value = lax.dot_general(probs_b, grads, rows, preferred_element_type=F32)
    dk_ref[...] = grad_key[:here]
    dv_ref[...] = grad_value[:here]
    far_ref[0] = grad_key[here:].astype(BF16)
    far_ref[1] = grad_value[here:].astype(BF16)


def attention_backward(at, queries, keys, values, hidden, weights, mask):
    here, features = queries.shape
    everywhere = keys.shape[0]
    heads = features // HD
    by_head = lambda rows: pl.BlockSpec((rows, HD), lambda h: (0, h))
    return pl.pallas_call(
        attention_kernel,
        grid=(heads,),
        in_specs=[SCALARS, by_head(here), by_head(everywhere), by_head(everywhere)]
        + [pl.BlockSpec(value.shape, lambda h: (0, 0)) for value in (*hidden, *weights, mask)],
        out_specs=[
            by_head(here),
            by_head(here),
            by_head(here),
            pl.BlockSpec((2, here, HD), lambda h: (0, 0, h)),
        ],
        out_shape=[
            jax.ShapeDtypeStruct((here, features), BF16),
            jax.ShapeDtypeStruct((here, features), F32),
            jax.ShapeDtypeStruct((here, features), F32),
            jax.ShapeDtypeStruct((2, here, features), BF16),
        ],
        scratch_shapes=[pltpu.VMEM((here, HD), BF16)],
        compiler_params=pltpu.CompilerParams(vmem_limit_bytes=32 * MIB),
    )(at, queries, keys, values, *hidden, *weights, mask)


def on_device(
    query,
    key_states,
    value_states,
    segment_ids,
    out_weight,
    grad_out,
    routes,
    route_gates,
    w_gate,
    w_up,
    w_down,
    saved_gate,
    saved_up,
):
    z_high, core, z_low = lax.axis_index("zh"), lax.axis_index("core"), lax.axis_index("zl")
    tokens = grad_out[0]

    at = jnp.stack([z_high, z_low, core]).astype(jnp.int32)

    half = TOK // 2
    blocks = {0: tokens}
    blocks[1], blocks[-1] = ring_shift(tokens, -1), ring_shift(tokens, 1)
    segment_chip = jnp.concatenate([segment_ids, swap(segment_ids, "core")], axis=0)
    table = route_table(routes, route_gates, segment_chip)
    blocks[1], blocks[-1], table, at = together(blocks[1], blocks[-1], table, at)

    blocks[2], blocks[-2] = ring_shift(blocks[1], -1), ring_shift(blocks[-1], 1)
    tables = lax.all_to_all(
        jnp.broadcast_to(table[None], (RING, 16, TOK)), RING_AXES, 0, 0, tiled=True
    )
    blocks[2], blocks[-2], tables, at = together(blocks[2], blocks[-2], tables, at)

    blocks[3], blocks[-3] = ring_shift(blocks[2], -1), ring_shift(blocks[-2], 1)
    saved_own, saved_leaving = split_saved(at, saved_gate[0], saved_up[0])
    blocks[3], blocks[-3], saved_leaving, at = together(
        blocks[3], blocks[-3], saved_leaving, at
    )

    last_up, last_down = ring_shift(blocks[3][:half], -1), ring_shift(blocks[-3][half:], 1)
    leaving_rows, collect_own = dispatch(at, tables, z_high, [blocks[i] for i in NEAR])
    last_up, last_down, saved_leaving, leaving_rows, at = together(
        last_up, last_down, saved_leaving, leaving_rows, at
    )
    blocks[4] = jnp.concatenate([last_up, last_down], axis=0)

    rows_own = plane_exchange(leaving_rows)
    saved_other = [swap(saved_leaving[0], "zh")]
    leaving_rows, collect_other = dispatch(at, tables, 1 - z_high, [blocks[i] for i in FAR])
    core_here, _ = together(core, last_up)
    heads_mine, heads_theirs = [], []
    for value in (query[0], key_states[0], value_states[0]):
        mine, theirs = own_features(value, core_here)
        heads_mine.append(mine)
        heads_theirs.append(theirs)
    arriving = swap(jnp.concatenate(heads_theirs, axis=1), "core")
    queries = jnp.concatenate([heads_mine[0], arriving[:, :512]], axis=0)
    key_value = jnp.concatenate(
        [jnp.concatenate(heads_mine[1:], axis=1), arriving[:, 512:]], axis=0
    )
    (
        rows_own,
        leaving_rows,
        saved_own,
        saved_other[0],
        saved_next,
        queries,
        key_value,
    ) = together(
        rows_own,
        leaving_rows,
        saved_own,
        saved_other[0],
        saved_leaving[1],
        queries,
        key_value,
    )

    rows_other = plane_exchange(leaving_rows)
    saved_other.append(swap(saved_next, "zh"))
    weights = []
    for weight in (w_down, w_gate, w_up):
        piece = jnp.swapaxes(weight[0], 0, 1)
        weights += [piece, swap(piece, "core")]
    leaving_own = expert_back(at, rows_own, [saved_own], weights)
    (
        rows_other,
        leaving_own,
        saved_other[1],
        saved_next,
        key_value,
    ) = together(
        rows_other,
        leaving_own,
        saved_other[1],
        saved_leaving[2],
        key_value,
    )

    back_own = plane_exchange(leaving_own)
    saved_other.append(swap(saved_next, "zh"))
    strip = out_weight.shape[0] // 4
    own_strip, saved_other[2] = together(
        lax.dynamic_slice_in_dim(out_weight, lax.axis_index("x") * strip, strip, axis=0),
        saved_other[2],
    )
    fetched = swap(own_strip, "zh")
    leaving = expert_back(at, rows_other, saved_other, weights)
    back_own, leaving, fetched, key_value = together(back_own, leaving, fetched, key_value)

    back_other = plane_exchange(leaving)
    key_value_far = swap(key_value, "zh")
    terms_own = combine(collect_own, back_own)
    table_far = lax.dynamic_index_in_dim(tables, (1 - z_high) * 4 + z_low, 0, keepdims=False)
    segment_keys = jnp.concatenate([table[8:10], table_far[8:10]], axis=0)
    segment_keys = segment_keys.astype(jnp.int32).reshape(4 * TOK)
    back_other, terms_own, key_value_far, segment_keys, fetched = together(
        back_other, terms_own, key_value_far, segment_keys, fetched
    )

    terms = ring_terms(at, collect_other, back_other, terms_own)
    middle = D // 2
    up = ring_shift(terms[4][:, :middle], 1)
    down = ring_shift(terms[4][:, middle:], -1)
    keys = jnp.concatenate([key_value[:, :512], key_value_far[:, :512]], axis=0)
    values = jnp.concatenate([key_value[:, 512:], key_value_far[:, 512:]], axis=0)
    offsets = jnp.arange(TOK, dtype=jnp.int32)
    place = lambda high, which: (high * 2 + which) * TOK + offsets
    chip_place = jnp.concatenate([place(z_high, core), place(z_high, 1 - core)])
    key_place = jnp.concatenate([chip_place, place(1 - z_high, core), place(1 - z_high, 1 - core)])
    segment_here = segment_keys[: 2 * TOK, None]
    causal = key_place[None, :] <= chip_place[:, None]
    image = (segment_here == segment_keys[None, :]) & (segment_here % 2 == 1)
    mask = (causal | image).astype(F32)
    pieces = [fetched]
    for distance in (1, 2, 3):
        pieces.append(lax.ppermute(fetched, "x", [((i + distance) % 4, i) for i in range(4)]))
    weight_far = lax.dynamic_slice_in_dim(
        jnp.concatenate(pieces + pieces[:3], axis=0),
        (4 - lax.axis_index("x")) % 4 * strip,
        4 * strip,
        axis=0,
    )
    up, down, keys, values, mask, weight_far = together(
        up, down, keys, values, mask, weight_far
    )
    terms = {step: value.astype(F32) for step, value in terms.items()}
    ahead, behind = terms[3], terms[-3]
    ahead = jnp.concatenate([ahead[:, :middle] + up.astype(F32), ahead[:, middle:]], axis=1)
    behind = jnp.concatenate([behind[:, :middle], behind[:, middle:] + down.astype(F32)], axis=1)
    for step in (2, 1, 0):
        ahead, behind = together(ahead.astype(BF16), behind.astype(BF16))
        up, down = together(ring_shift(ahead, 1), ring_shift(behind, -1))
        if step > 0:
            ahead = terms[step] + up.astype(F32)
            behind = terms[-step] + down.astype(F32)
    summed = tokens.astype(F32) + terms[0] + up.astype(F32) + down.astype(F32)
    d_hidden = summed.astype(BF16)

    grad_query, grad_key, grad_value, far = attention_backward(
        at,
        queries,
        keys,
        values,
        (d_hidden, swap(d_hidden, "core")),
        (out_weight, weight_far),
        mask,
    )
    far_theirs = swap(far[:, TOK:], "core")
    far_full = jnp.stack([all_features(far[i, :TOK], far_theirs[i], core) for i in range(2)])
    arrived = swap(far_full, "zh").astype(F32)
    near = [
        all_features(grad[:TOK], swap(grad[TOK:], "core"), core)
        for grad in (grad_query, grad_key, grad_value)
    ]
    return (
        d_hidden[None],
        near[0][None],
        (near[1] + arrived[0]).astype(BF16)[None],
        (near[2] + arrived[1]).astype(BF16)[None],
    )


def solution(mesh):
    fine = Mesh(mesh.devices.reshape(2, 2, 4, 4, 4), ("zh", "core", "x", "y", "zl"))
    exp = ("x", "y", "zl")
    ctx = ("zh", "core")
    in_specs = (
        P(exp, ctx, None),
        P(exp, ctx, None),
        P(exp, ctx, None),
        P(exp, ctx),
        P(ctx, None),
        P(exp, ctx, None),
        P(exp, ctx, None),
        P(exp, ctx, None),
        P(exp, None, ctx),
        P(exp, None, ctx),
        P(exp, None, ctx),
        P(exp, ctx, None),
        P(exp, ctx, None),
    )
    out_specs = (P(exp, ctx, None),) * 4
    return jax.shard_map(
        on_device, mesh=fine, in_specs=in_specs, out_specs=out_specs, check_vma=False
    )
```

```python
import functools
import math

import jax
import jax.numpy as jnp
from jax import lax
from jax.experimental import pallas as pl
from jax.experimental.pallas import tpu as pltpu
from jax.sharding import Mesh
from jax.sharding import PartitionSpec as P

D = 2048
HEADS = 8
HD = 128
EXPERTS = 64
CAP = 10
TOK = 128
RING = 8
RING_AXES = ("zh", "zl")
PLANE_AXES = ("x", "y")
PLANE = 16
HALF_ROWS = EXPERTS * CAP
F32 = jnp.float32
BF16 = jnp.bfloat16


def ring_shift(value, step):
    return lax.ppermute(value, RING_AXES, [(i, (i + step) % RING) for i in range(RING)])


def swap(value, axis):
    return lax.ppermute(value, axis, [(0, 1), (1, 0)])


def plane_exchange(rows):
    width = rows.shape[1]
    return lax.all_to_all(
        rows.reshape(PLANE, HALF_ROWS // PLANE, width), PLANE_AXES, 0, 0, tiled=True
    ).reshape(HALF_ROWS, width)


def together(*values):
    return lax.optimization_barrier(values)


def route_table(routes, route_gates, segments):
    ids = routes[0]
    experts = jnp.arange(EXPERTS, dtype=jnp.int32)
    named = (ids[:, :, None] == experts).astype(F32)
    table = jnp.sum(named, axis=1)
    position = jnp.arange(TOK, dtype=jnp.int32)
    earlier = (position[None, :] < position[:, None]).astype(BF16)
    before = jnp.dot(earlier, table.astype(BF16), preferred_element_type=F32)
    slot = jnp.sum(named * before[:, None, :], axis=2)
    codes = ids.astype(F32) * 16.0 + slot
    spare = jnp.zeros((6, TOK), F32)
    return jnp.concatenate([codes.T, route_gates[0].T, segments.astype(F32), spare], axis=0)


NEAR = (-3, -2, -1, 0, 1, 2, 3)
FAR = (1, 2, 3, 4, -3, -2, -1)
SAVED_ROWS = (256, 256, 128)
SAVED_BLOCK = 128
MIB = 1024 * 1024


SCALARS = pl.BlockSpec(memory_space=pltpu.SMEM)


def saved_kernel(at_ref, gate_ref, up_ref, own_ref, *outs):
    units = gate_ref.shape[1] // 2
    step = pl.program_id(0)
    first = 0
    for high in range(2):

        @pl.when(at_ref[0] == high)
        def _():
            mine = slice(high * units, (high + 1) * units)
            own_ref[:, :units] = gate_ref[:, mine]
            own_ref[:, units:] = up_ref[:, mine]

    for ref, rows in zip(outs, SAVED_ROWS):
        for high in range(2):

            @pl.when((at_ref[0] == high) & (step >= first) & (step < first + rows // SAVED_BLOCK))
            def _():
                other = slice((1 - high) * units, (2 - high) * units)
                ref[:, :units] = gate_ref[:, other]
                ref[:, units:] = up_ref[:, other]

        first += rows // SAVED_BLOCK


def split_saved(at, saved_gate, saved_up):
    width = saved_gate.shape[1]
    by_rows = pl.BlockSpec((SAVED_BLOCK, width), lambda i: (i, 0))
    parts, shapes, first = [], [], 0
    for rows in SAVED_ROWS:
        count = rows // SAVED_BLOCK
        parts.append(
            pl.BlockSpec(
                (SAVED_BLOCK, width),
                lambda i, first=first, count=count: (jnp.clip(i - first, 0, count - 1), 0),
            )
        )
        shapes.append(jax.ShapeDtypeStruct((rows, width), BF16))
        first += count
    own, *other = pl.pallas_call(
        saved_kernel,
        grid=(HALF_ROWS // SAVED_BLOCK,),
        in_specs=[SCALARS, by_rows, by_rows],
        out_specs=[by_rows, *parts],
        out_shape=[jax.ShapeDtypeStruct(saved_gate.shape, BF16), *shapes],
        compiler_params=pltpu.CompilerParams(vmem_limit_bytes=24 * MIB),
    )(at, saved_gate, saved_up)
    return own, other


def placement_kernel(at_ref, tables_ref, *outs):
    numbers = lax.broadcasted_iota(jnp.int32, (HALF_ROWS, TOK), 0)
    for which in range(2):
        select_ref, collect_ref, gate_ref = outs[3 * which : 3 * which + 3]
        first = 4 * (at_ref[0] if which == 0 else 1 - at_ref[0])
        total = jnp.zeros((HALF_ROWS, 1), F32)
        for source in range(4):
            table = tables_ref[first + source]
            codes = table[:4].astype(jnp.int32)
            expert = codes >> 4
            row = (expert >> 2) * (4 * CAP) + source * CAP + (codes & 15)
            row = jnp.where((expert & 3) == at_ref[1], row, -1)
            marks = jnp.zeros((HALF_ROWS, TOK), F32)
            gates = jnp.zeros((HALF_ROWS, TOK), F32)
            for choice in range(4):
                hit = numbers == row[choice : choice + 1]
                marks = jnp.where(hit, 1.0, marks)
                gates = jnp.where(hit, table[4 + choice : 5 + choice], gates)
            columns = slice(source * TOK, (source + 1) * TOK)
            select_ref[:, columns] = marks.astype(BF16)
            collect_ref[columns, :] = marks.T.astype(BF16)
            total = total + jnp.sum(gates, axis=1, keepdims=True)
        gate_ref[...] = total


def placement(at, tables):
    shapes = [
        jax.ShapeDtypeStruct((HALF_ROWS, 4 * TOK), BF16),
        jax.ShapeDtypeStruct((4 * TOK, HALF_ROWS), BF16),
        jax.ShapeDtypeStruct((HALF_ROWS, 1), F32),
    ] * 2
    outs = pl.pallas_call(
        placement_kernel,
        grid=(1,),
        in_specs=[SCALARS, pl.BlockSpec(tables.shape, lambda j: (0, 0, 0))],
        out_specs=[pl.BlockSpec(shape.shape, lambda j: (0, 0)) for shape in shapes],
        out_shape=shapes,
        compiler_params=pltpu.CompilerParams(vmem_limit_bytes=24 * MIB),
    )(at, tables)
    return outs[:3], outs[3:]


def dispatch_kernel(at_ref, select_ref, gate_ref, *refs):
    blocks, rows_ref, tokens = refs[:7], refs[7], refs[8]
    for low in range(4):

        @pl.when(at_ref[1] == low)
        def _():
            for source in range(4):
                tokens[source * TOK : (source + 1) * TOK, :] = blocks[source + 3 - low][...]

    picked = jnp.dot(select_ref[...], tokens[...], preferred_element_type=F32)
    rows_ref[...] = (picked * gate_ref[...]).astype(BF16)


def dispatch(at, select, row_gate, blocks):
    width = 512
    return pl.pallas_call(
        dispatch_kernel,
        grid=(D // width,),
        in_specs=[
            SCALARS,
            pl.BlockSpec(select.shape, lambda j: (0, 0)),
            pl.BlockSpec(row_gate.shape, lambda j: (0, 0)),
        ]
        + [pl.BlockSpec((TOK, width), lambda j: (0, j))] * 7,
        out_specs=pl.BlockSpec((HALF_ROWS, width), lambda j: (0, j)),
        out_shape=pltpu.HBM((HALF_ROWS, D), BF16),
        scratch_shapes=[pltpu.VMEM((4 * TOK, width), BF16)],
        compiler_params=pltpu.CompilerParams(vmem_limit_bytes=40 * MIB),
    )(at, select, row_gate, *blocks)


def expert_kernel(at_ref, *refs, parts):
    rows_hbm, saved_hbm = refs[0], refs[1 : 1 + parts]
    weights, refs = refs[1 + parts : 7 + parts], refs[7 + parts :]
    out_ref, rows_ref, saved, down, gate, up, grad_gate, grad_up, sems = refs
    piece = weights[0].shape[0]
    units = 2 * piece
    step = pl.program_id(0)
    width = out_ref.shape[1]

    @pl.when(step == 0)
    def _():
        copies = []
        for number, ref in enumerate(weights):
            where = at_ref[2] if number % 2 == 0 else 1 - at_ref[2]
            start = pl.multiple_of(where * piece, 16)
            target = (down, gate, up)[number // 2].at[pl.ds(start, piece), :]
            copies.append(pltpu.make_async_copy(ref, target, sems.at[number]))
        needed = [pltpu.make_async_copy(rows_hbm, rows_ref, sems.at[6])]
        first = 0
        for number, ref in enumerate(saved_hbm):
            target = saved.at[pl.ds(first, ref.shape[0]), :]
            needed.append(pltpu.make_async_copy(ref, target, sems.at[7 + number]))
            first += ref.shape[0]
        for copy in (*copies[:2], *needed, *copies[2:]):
            copy.start()
        for copy in (*copies[:2], *needed):
            copy.wait()
        for first in range(0, HALF_ROWS, 320):
            rows = slice(first, first + 320)
            hidden_grad = lax.dot_general(
                rows_ref[rows, :],
                down[...],
                (((1,), (1,)), ((), ())),
                preferred_element_type=F32,
            )
            gate_pre = saved[rows, :units].astype(F32)
            up_pre = saved[rows, units:].astype(F32)
            sigmoid_gate = jax.nn.sigmoid(gate_pre)
            grad_gate[rows, :] = (
                hidden_grad * up_pre * sigmoid_gate * (1.0 + gate_pre * (1.0 - sigmoid_gate))
            ).astype(BF16)
            grad_up[rows, :] = (hidden_grad * gate_pre * sigmoid_gate).astype(BF16)
        for copy in copies[2:]:
            copy.wait()

    columns = pl.ds(pl.multiple_of(step * width, 128), width)
    total = jnp.dot(grad_gate[...], gate[:, columns], preferred_element_type=F32)
    total = total + jnp.dot(grad_up[...], up[:, columns], preferred_element_type=F32)
    out_ref[...] = total.astype(BF16)


def expert_back(at, rows, saved, weights):
    width = 512
    units = saved[0].shape[1] // 2
    return pl.pallas_call(
        functools.partial(expert_kernel, parts=len(saved)),
        grid=(D // width,),
        in_specs=[SCALARS]
        + [pl.BlockSpec(memory_space=pltpu.HBM)] * (1 + len(saved))
        + [pl.BlockSpec(memory_space=pl.ANY)] * len(weights),
        out_specs=pl.BlockSpec((HALF_ROWS, width), lambda j: (0, j)),
        out_shape=pltpu.HBM((HALF_ROWS, D), BF16),
        scratch_shapes=[pltpu.VMEM((HALF_ROWS, D), BF16), pltpu.VMEM((HALF_ROWS, 2 * units), BF16)]
        + [pltpu.VMEM((units, D), BF16)] * 3
        + [pltpu.VMEM((HALF_ROWS, units), BF16)] * 2
        + [pltpu.SemaphoreType.DMA((7 + len(saved),))],
        compiler_params=pltpu.CompilerParams(vmem_limit_bytes=48 * MIB),
    )(at, rows, *saved, *weights)


def combine(collect, returned):
    return jnp.dot(collect, returned, preferred_element_type=F32).astype(BF16)


RING_STEPS = (4, 3, -3, 2, -2, 1, -1, 0)


def terms_kernel(at_ref, collect_hbm, back_hbm, own_hbm, *refs):
    outs, (collect, back, own, other, sems) = refs[: len(RING_STEPS)], refs[len(RING_STEPS) :]
    j = pl.program_id(0)
    width = other.shape[1]
    columns = pl.ds(pl.multiple_of(j * width, 128), width)
    arrivals = []
    for part in range(back_hbm.shape[1] // width):
        at_part = pl.ds(part * width, width)
        arrivals.append(
            pltpu.make_async_copy(back_hbm.at[:, at_part], back.at[:, at_part], sems.at[part])
        )
    others = [
        pltpu.make_async_copy(collect_hbm, collect, sems.at[len(arrivals)]),
        pltpu.make_async_copy(own_hbm, own, sems.at[len(arrivals) + 1]),
    ]

    @pl.when(j == 0)
    def _():
        for copy in (others[0], arrivals[0], others[1], *arrivals[1:]):
            copy.start()
        for copy in others:
            copy.wait()

    for part, copy in enumerate(arrivals):

        @pl.when(j == part)
        def _():
            copy.wait()

    other[...] = combine(collect[...], back[:, columns])
    for step, out in zip(RING_STEPS, outs):
        target = (at_ref[0] * 4 + at_ref[1] + step + RING) % RING
        rows = pl.ds(pl.multiple_of((target % 4) * TOK, TOK), TOK)
        out[...] = jnp.where(target // 4 == at_ref[0], own[rows, columns], other[rows, :])


def ring_terms(at, collect_other, back_other, terms_own):
    width = 512
    rows, slots = collect_other.shape
    outs = pl.pallas_call(
        terms_kernel,
        grid=(D // width,),
        in_specs=[SCALARS] + [pl.BlockSpec(memory_space=pltpu.HBM)] * 3,
        out_specs=[pl.BlockSpec((TOK, width), lambda j: (0, j))] * len(RING_STEPS),
        out_shape=[jax.ShapeDtypeStruct((TOK, D), BF16)] * len(RING_STEPS),
        scratch_shapes=[
            pltpu.VMEM((rows, slots), BF16),
            pltpu.VMEM((slots, D), BF16),
            pltpu.VMEM((rows, D), BF16),
            pltpu.VMEM((rows, width), BF16),
            pltpu.SemaphoreType.DMA((D // width + 2,)),
        ],
        compiler_params=pltpu.CompilerParams(vmem_limit_bytes=40 * MIB),
    )(at, collect_other, back_other, terms_own)
    return dict(zip(RING_STEPS, outs))


def own_features(value, core):
    a, b, c, d = (value[..., 256 * i : 256 * (i + 1)] for i in range(4))
    first = core == 0
    mine = jnp.concatenate([jnp.where(first, a, b), jnp.where(first, c, d)], axis=-1)
    theirs = jnp.concatenate([jnp.where(first, b, a), jnp.where(first, d, c)], axis=-1)
    return mine, theirs


def all_features(mine, theirs, core):
    first = core == 0
    low, high = slice(0, 256), slice(256, 512)
    return jnp.concatenate(
        [
            jnp.where(first, mine[:, low], theirs[:, low]),
            jnp.where(first, theirs[:, low], mine[:, low]),
            jnp.where(first, mine[:, high], theirs[:, high]),
            jnp.where(first, theirs[:, high], mine[:, high]),
        ],
        axis=1,
    )


def attention_kernel(
    at_ref,
    q_ref,
    k_ref,
    v_ref,
    near_hidden_ref,
    far_hidden_ref,
    near_weight_ref,
    far_weight_ref,
    mask_ref,
    dq_ref,
    dk_ref,
    dv_ref,
    far_ref,
    grads_ref,
):
    scale = 1.0 / math.sqrt(HD)
    here = q_ref.shape[0]
    head = pl.program_id(0)
    queries, keys, values = q_ref[...], k_ref[...], v_ref[...]
    last = (((1,), (1,)), ((), ()))
    rows_here = pl.ds(pl.multiple_of((head % 2) * HD, HD), HD)
    weight = jnp.where(
        head // 2 == at_ref[0], near_weight_ref[rows_here, :], far_weight_ref[rows_here, :]
    )
    for number, ref in enumerate((near_hidden_ref, far_hidden_ref)):
        grads_ref[number * TOK : (number + 1) * TOK, :] = lax.dot_general(
            ref[...], weight, last, preferred_element_type=F32
        ).astype(BF16)
    grads = grads_ref[...]
    rows = (((0,), (0,)), ((), ()))
    scores = lax.dot_general(queries, keys, last, preferred_element_type=F32) * scale
    scores = jnp.where(mask_ref[...] > 0.0, scores, -jnp.inf)
    expd = jnp.exp(scores - jnp.max(scores, axis=1, keepdims=True))
    probs = expd / jnp.sum(expd, axis=1, keepdims=True)
    probs_b = probs.astype(BF16)
    attn_out = jnp.dot(probs_b, values, preferred_element_type=F32)
    delta = jnp.sum(grads.astype(F32) * attn_out, axis=1, keepdims=True)
    dprobs = lax.dot_general(grads, values, last, preferred_element_type=F32)
    dscores = (probs * (dprobs - delta)).astype(BF16)
    dq_ref[...] = (jnp.dot(dscores, keys, preferred_element_type=F32) * scale).astype(BF16)
    grad_key = lax.dot_general(dscores, queries, rows, preferred_element_type=F32) * scale
    grad_value = lax.dot_general(probs_b, grads, rows, preferred_element_type=F32)
    dk_ref[...] = grad_key[:here]
    dv_ref[...] = grad_value[:here]
    far_ref[0] = grad_key[here:].astype(BF16)
    far_ref[1] = grad_value[here:].astype(BF16)


def attention_backward(at, queries, keys, values, hidden, weights, mask):
    here, features = queries.shape
    everywhere = keys.shape[0]
    heads = features // HD
    by_head = lambda rows: pl.BlockSpec((rows, HD), lambda h: (0, h))
    return pl.pallas_call(
        attention_kernel,
        grid=(heads,),
        in_specs=[SCALARS, by_head(here), by_head(everywhere), by_head(everywhere)]
        + [pl.BlockSpec(value.shape, lambda h: (0, 0)) for value in (*hidden, *weights, mask)],
        out_specs=[
            by_head(here),
            by_head(here),
            by_head(here),
            pl.BlockSpec((2, here, HD), lambda h: (0, 0, h)),
        ],
        out_shape=[
            jax.ShapeDtypeStruct((here, features), BF16),
            jax.ShapeDtypeStruct((here, features), F32),
            jax.ShapeDtypeStruct((here, features), F32),
            jax.ShapeDtypeStruct((2, here, features), BF16),
        ],
        scratch_shapes=[pltpu.VMEM((here, HD), BF16)],
        compiler_params=pltpu.CompilerParams(vmem_limit_bytes=32 * MIB),
    )(at, queries, keys, values, *hidden, *weights, mask)


def on_device(
    query,
    key_states,
    value_states,
    segment_ids,
    out_weight,
    grad_out,
    routes,
    route_gates,
    w_gate,
    w_up,
    w_down,
    saved_gate,
    saved_up,
):
    z_high, core, z_low = lax.axis_index("zh"), lax.axis_index("core"), lax.axis_index("zl")
    tokens = grad_out[0]

    at = jnp.stack([z_high, z_low, core]).astype(jnp.int32)

    half = TOK // 2
    blocks = {0: tokens}
    blocks[1], blocks[-1] = ring_shift(tokens, -1), ring_shift(tokens, 1)
    segment_chip = jnp.concatenate([segment_ids, swap(segment_ids, "core")], axis=0)
    table = route_table(routes, route_gates, segment_chip)
    saved_own, saved_leaving = split_saved(at, saved_gate[0], saved_up[0])
    blocks[1], blocks[-1], table, at, saved_leaving = together(
        blocks[1], blocks[-1], table, at, saved_leaving
    )

    blocks[2], blocks[-2] = ring_shift(blocks[1], -1), ring_shift(blocks[-1], 1)
    tables = lax.all_to_all(
        jnp.broadcast_to(table[None], (RING, 16, TOK)), RING_AXES, 0, 0, tiled=True
    )
    blocks[2], blocks[-2], tables, at = together(blocks[2], blocks[-2], tables, at)

    blocks[3], blocks[-3] = ring_shift(blocks[2], -1), ring_shift(blocks[-2], 1)
    place_own, place_other = placement(at, tables)
    blocks[3], blocks[-3], place_own, place_other, at = together(
        blocks[3], blocks[-3], place_own, place_other, at
    )
    select_own, collect_own, gate_own = place_own
    select_other, collect_other, gate_other = place_other

    last_up, last_down = ring_shift(blocks[3][:half], -1), ring_shift(blocks[-3][half:], 1)
    leaving_rows = dispatch(at, select_own, gate_own, [blocks[i] for i in NEAR])
    last_up, last_down, saved_leaving, leaving_rows, at = together(
        last_up, last_down, saved_leaving, leaving_rows, at
    )
    blocks[4] = jnp.concatenate([last_up, last_down], axis=0)

    rows_own = plane_exchange(leaving_rows)
    saved_other = [swap(saved_leaving[0], "zh")]
    leaving_rows = dispatch(at, select_other, gate_other, [blocks[i] for i in FAR])
    core_here, _ = together(core, last_up)
    heads_mine, heads_theirs = [], []
    for value in (query[0], key_states[0], value_states[0]):
        mine, theirs = own_features(value, core_here)
        heads_mine.append(mine)
        heads_theirs.append(theirs)
    arriving = swap(jnp.concatenate(heads_theirs, axis=1), "core")
    queries = jnp.concatenate([heads_mine[0], arriving[:, :512]], axis=0)
    key_value = jnp.concatenate(
        [jnp.concatenate(heads_mine[1:], axis=1), arriving[:, 512:]], axis=0
    )
    (
        rows_own,
        leaving_rows,
        saved_own,
        saved_other[0],
        saved_next,
        queries,
        key_value,
    ) = together(
        rows_own,
        leaving_rows,
        saved_own,
        saved_other[0],
        saved_leaving[1],
        queries,
        key_value,
    )

    rows_other = plane_exchange(leaving_rows)
    saved_other.append(swap(saved_next, "zh"))
    weights = []
    for weight in (w_down, w_gate, w_up):
        piece = jnp.swapaxes(weight[0], 0, 1)
        weights += [piece, swap(piece, "core")]
    leaving_own = expert_back(at, rows_own, [saved_own], weights)
    (
        rows_other,
        leaving_own,
        saved_other[1],
        saved_next,
        key_value,
    ) = together(
        rows_other,
        leaving_own,
        saved_other[1],
        saved_leaving[2],
        key_value,
    )

    back_own = plane_exchange(leaving_own)
    saved_other.append(swap(saved_next, "zh"))
    strip = out_weight.shape[0] // 4
    own_strip = lax.dynamic_slice_in_dim(out_weight, lax.axis_index("x") * strip, strip, axis=0)
    leaving = expert_back(at, rows_other, saved_other, weights)
    back_own, leaving, own_strip, key_value = together(back_own, leaving, own_strip, key_value)

    back_other = plane_exchange(leaving)
    key_value_far = swap(key_value, "zh")
    terms_own = combine(collect_own, back_own)
    table_far = lax.dynamic_index_in_dim(tables, (1 - z_high) * 4 + z_low, 0, keepdims=False)
    segment_keys = jnp.concatenate([table[8:10], table_far[8:10]], axis=0)
    segment_keys = segment_keys.astype(jnp.int32).reshape(4 * TOK)
    fetched = swap(own_strip, "zh")
    back_other, terms_own, key_value_far, segment_keys, fetched = together(
        back_other, terms_own, key_value_far, segment_keys, fetched
    )

    terms = ring_terms(at, collect_other, back_other, terms_own)
    middle = D // 2
    up = ring_shift(terms[4][:, :middle], 1)
    down = ring_shift(terms[4][:, middle:], -1)
    keys = jnp.concatenate([key_value[:, :512], key_value_far[:, :512]], axis=0)
    values = jnp.concatenate([key_value[:, 512:], key_value_far[:, 512:]], axis=0)
    offsets = jnp.arange(TOK, dtype=jnp.int32)
    place = lambda high, which: (high * 2 + which) * TOK + offsets
    chip_place = jnp.concatenate([place(z_high, core), place(z_high, 1 - core)])
    key_place = jnp.concatenate([chip_place, place(1 - z_high, core), place(1 - z_high, 1 - core)])
    segment_here = segment_keys[: 2 * TOK, None]
    causal = key_place[None, :] <= chip_place[:, None]
    image = (segment_here == segment_keys[None, :]) & (segment_here % 2 == 1)
    mask = (causal | image).astype(F32)
    pieces = [fetched]
    for distance in (1, 2, 3):
        pieces.append(lax.ppermute(fetched, "x", [((i + distance) % 4, i) for i in range(4)]))
    weight_far = lax.dynamic_slice_in_dim(
        jnp.concatenate(pieces + pieces[:3], axis=0),
        (4 - lax.axis_index("x")) % 4 * strip,
        4 * strip,
        axis=0,
    )
    up, down, keys, values, mask, weight_far = together(
        up, down, keys, values, mask, weight_far
    )
    terms = {step: value.astype(F32) for step, value in terms.items()}
    ahead, behind = terms[3], terms[-3]
    ahead = jnp.concatenate([ahead[:, :middle] + up.astype(F32), ahead[:, middle:]], axis=1)
    behind = jnp.concatenate([behind[:, :middle], behind[:, middle:] + down.astype(F32)], axis=1)
    for step in (2, 1, 0):
        ahead, behind = together(ahead.astype(BF16), behind.astype(BF16))
        up, down = together(ring_shift(ahead, 1), ring_shift(behind, -1))
        if step > 0:
            ahead = terms[step] + up.astype(F32)
            behind = terms[-step] + down.astype(F32)
    summed = tokens.astype(F32) + terms[0] + up.astype(F32) + down.astype(F32)
    d_hidden = summed.astype(BF16)

    grad_query, grad_key, grad_value, far = attention_backward(
        at,
        queries,
        keys,
        values,
        (d_hidden, swap(d_hidden, "core")),
        (out_weight, weight_far),
        mask,
    )
    far_theirs = swap(far[:, TOK:], "core")
    far_full = jnp.stack([all_features(far[i, :TOK], far_theirs[i], core) for i in range(2)])
    arrived = swap(far_full, "zh").astype(F32)
    near = [
        all_features(grad[:TOK], swap(grad[TOK:], "core"), core)
        for grad in (grad_query, grad_key, grad_value)
    ]
    return (
        d_hidden[None],
        near[0][None],
        (near[1] + arrived[0]).astype(BF16)[None],
        (near[2] + arrived[1]).astype(BF16)[None],
    )


def solution(mesh):
    fine = Mesh(mesh.devices.reshape(2, 2, 4, 4, 4), ("zh", "core", "x", "y", "zl"))
    exp = ("x", "y", "zl")
    ctx = ("zh", "core")
    in_specs = (
        P(exp, ctx, None),
        P(exp, ctx, None),
        P(exp, ctx, None),
        P(exp, ctx),
        P(ctx, None),
        P(exp, ctx, None),
        P(exp, ctx, None),
        P(exp, ctx, None),
        P(exp, None, ctx),
        P(exp, None, ctx),
        P(exp, None, ctx),
        P(exp, ctx, None),
        P(exp, ctx, None),
    )
    out_specs = (P(exp, ctx, None),) * 4
    return jax.shard_map(
        on_device, mesh=fine, in_specs=in_specs, out_specs=out_specs, check_vma=False
    )
```

```python
import functools
import math

import jax
import jax.numpy as jnp
from jax import lax
from jax.experimental import pallas as pl
from jax.experimental.pallas import tpu as pltpu
from jax.sharding import Mesh
from jax.sharding import PartitionSpec as P

D = 2048
HEADS = 8
HD = 128
EXPERTS = 64
CAP = 10
TOK = 128
RING = 8
RING_AXES = ("zh", "zl")
PLANE_AXES = ("x", "y")
PLANE = 16
HALF_ROWS = EXPERTS * CAP
F32 = jnp.float32
BF16 = jnp.bfloat16


def ring_shift(value, step):
    return lax.ppermute(value, RING_AXES, [(i, (i + step) % RING) for i in range(RING)])


def swap(value, axis):
    return lax.ppermute(value, axis, [(0, 1), (1, 0)])


def plane_exchange(rows):
    width = rows.shape[1]
    return lax.all_to_all(
        rows.reshape(PLANE, HALF_ROWS // PLANE, width), PLANE_AXES, 0, 0, tiled=True
    ).reshape(HALF_ROWS, width)


def together(*values):
    return lax.optimization_barrier(values)


def route_table(routes, route_gates, segments):
    ids = routes[0]
    experts = jnp.arange(EXPERTS, dtype=jnp.int32)
    named = (ids[:, :, None] == experts).astype(F32)
    table = jnp.sum(named, axis=1)
    position = jnp.arange(TOK, dtype=jnp.int32)
    earlier = (position[None, :] < position[:, None]).astype(BF16)
    before = jnp.dot(earlier, table.astype(BF16), preferred_element_type=F32)
    slot = jnp.sum(named * before[:, None, :], axis=2)
    codes = ids.astype(F32) * 16.0 + slot
    spare = jnp.zeros((6, TOK), F32)
    return jnp.concatenate([codes.T, route_gates[0].T, segments.astype(F32), spare], axis=0)


NEAR = (-3, -2, -1, 0, 1, 2, 3)
FAR = (1, 2, 3, 4, -3, -2, -1)
SAVED_ROWS = (256, 256, 128)
SAVED_BLOCK = 128
MIB = 1024 * 1024


SCALARS = pl.BlockSpec(memory_space=pltpu.SMEM)


def saved_kernel(at_ref, gate_ref, up_ref, own_ref, *outs):
    units = gate_ref.shape[1] // 2
    step = pl.program_id(0)
    first = 0
    for high in range(2):

        @pl.when(at_ref[0] == high)
        def _():
            mine = slice(high * units, (high + 1) * units)
            own_ref[:, :units] = gate_ref[:, mine]
            own_ref[:, units:] = up_ref[:, mine]

    for ref, rows in zip(outs, SAVED_ROWS):
        for high in range(2):

            @pl.when((at_ref[0] == high) & (step >= first) & (step < first + rows // SAVED_BLOCK))
            def _():
                other = slice((1 - high) * units, (2 - high) * units)
                ref[:, :units] = gate_ref[:, other]
                ref[:, units:] = up_ref[:, other]

        first += rows // SAVED_BLOCK


def split_saved(at, saved_gate, saved_up):
    width = saved_gate.shape[1]
    by_rows = pl.BlockSpec((SAVED_BLOCK, width), lambda i: (i, 0))
    parts, shapes, first = [], [], 0
    for rows in SAVED_ROWS:
        count = rows // SAVED_BLOCK
        parts.append(
            pl.BlockSpec(
                (SAVED_BLOCK, width),
                lambda i, first=first, count=count: (jnp.clip(i - first, 0, count - 1), 0),
            )
        )
        shapes.append(jax.ShapeDtypeStruct((rows, width), BF16))
        first += count
    own, *other = pl.pallas_call(
        saved_kernel,
        grid=(HALF_ROWS // SAVED_BLOCK,),
        in_specs=[SCALARS, by_rows, by_rows],
        out_specs=[by_rows, *parts],
        out_shape=[jax.ShapeDtypeStruct(saved_gate.shape, BF16), *shapes],
        compiler_params=pltpu.CompilerParams(vmem_limit_bytes=24 * MIB),
    )(at, saved_gate, saved_up)
    return own, other


def placement_kernel(at_ref, tables_ref, *outs):
    numbers = lax.broadcasted_iota(jnp.int32, (HALF_ROWS, TOK), 0)
    for which in range(2):
        select_ref, collect_ref, gate_ref = outs[3 * which : 3 * which + 3]
        first = 4 * (at_ref[0] if which == 0 else 1 - at_ref[0])
        total = jnp.zeros((HALF_ROWS, 1), F32)
        for source in range(4):
            table = tables_ref[first + source]
            codes = table[:4].astype(jnp.int32)
            expert = codes >> 4
            row = (expert >> 2) * (4 * CAP) + source * CAP + (codes & 15)
            row = jnp.where((expert & 3) == at_ref[1], row, -1)
            marks = jnp.zeros((HALF_ROWS, TOK), F32)
            gates = jnp.zeros((HALF_ROWS, TOK), F32)
            for choice in range(4):
                hit = numbers == row[choice : choice + 1]
                marks = jnp.where(hit, 1.0, marks)
                gates = jnp.where(hit, table[4 + choice : 5 + choice], gates)
            columns = slice(source * TOK, (source + 1) * TOK)
            select_ref[:, columns] = marks.astype(BF16)
            collect_ref[columns, :] = marks.T.astype(BF16)
            total = total + jnp.sum(gates, axis=1, keepdims=True)
        gate_ref[...] = total


def placement(at, tables):
    shapes = [
        jax.ShapeDtypeStruct((HALF_ROWS, 4 * TOK), BF16),
        jax.ShapeDtypeStruct((4 * TOK, HALF_ROWS), BF16),
        jax.ShapeDtypeStruct((HALF_ROWS, 1), F32),
    ] * 2
    outs = pl.pallas_call(
        placement_kernel,
        grid=(1,),
        in_specs=[SCALARS, pl.BlockSpec(tables.shape, lambda j: (0, 0, 0))],
        out_specs=[pl.BlockSpec(shape.shape, lambda j: (0, 0)) for shape in shapes],
        out_shape=shapes,
        compiler_params=pltpu.CompilerParams(vmem_limit_bytes=24 * MIB),
    )(at, tables)
    return outs[:3], outs[3:]


def dispatch_kernel(at_ref, select_ref, gate_ref, *refs):
    blocks, rows_ref, tokens = refs[:7], refs[7], refs[8]
    for low in range(4):

        @pl.when(at_ref[1] == low)
        def _():
            for source in range(4):
                tokens[source * TOK : (source + 1) * TOK, :] = blocks[source + 3 - low][...]

    picked = jnp.dot(select_ref[...], tokens[...], preferred_element_type=F32)
    rows_ref[...] = (picked * gate_ref[...]).astype(BF16)


def dispatch(at, select, row_gate, blocks):
    width = 512
    return pl.pallas_call(
        dispatch_kernel,
        grid=(D // width,),
        in_specs=[
            SCALARS,
            pl.BlockSpec(select.shape, lambda j: (0, 0)),
            pl.BlockSpec(row_gate.shape, lambda j: (0, 0)),
        ]
        + [pl.BlockSpec((TOK, width), lambda j: (0, j))] * 7,
        out_specs=pl.BlockSpec((HALF_ROWS, width), lambda j: (0, j)),
        out_shape=pltpu.HBM((HALF_ROWS, D), BF16),
        scratch_shapes=[pltpu.VMEM((4 * TOK, width), BF16)],
        compiler_params=pltpu.CompilerParams(vmem_limit_bytes=40 * MIB),
    )(at, select, row_gate, *blocks)


def expert_kernel(at_ref, *refs, parts):
    rows_hbm, saved_hbm = refs[0], refs[1 : 1 + parts]
    weights, refs = refs[1 + parts : 7 + parts], refs[7 + parts :]
    out_ref, rows_ref, saved, down, gate, up, grad_gate, grad_up, sems = refs
    piece = weights[0].shape[0]
    units = 2 * piece
    step = pl.program_id(0)
    width = out_ref.shape[1]

    @pl.when(step == 0)
    def _():
        copies = []
        for number, ref in enumerate(weights):
            where = at_ref[2] if number % 2 == 0 else 1 - at_ref[2]
            start = pl.multiple_of(where * piece, 16)
            target = (down, gate, up)[number // 2].at[pl.ds(start, piece), :]
            copies.append(pltpu.make_async_copy(ref, target, sems.at[number]))
        needed = [pltpu.make_async_copy(rows_hbm, rows_ref, sems.at[6])]
        first = 0
        for number, ref in enumerate(saved_hbm):
            target = saved.at[pl.ds(first, ref.shape[0]), :]
            needed.append(pltpu.make_async_copy(ref, target, sems.at[7 + number]))
            first += ref.shape[0]
        for copy in (*copies[:2], *needed, *copies[2:]):
            copy.start()
        for copy in (*copies[:2], *needed):
            copy.wait()
        for first in range(0, HALF_ROWS, 320):
            rows = slice(first, first + 320)
            hidden_grad = lax.dot_general(
                rows_ref[rows, :],
                down[...],
                (((1,), (1,)), ((), ())),
                preferred_element_type=F32,
            )
            gate_pre = saved[rows, :units].astype(F32)
            up_pre = saved[rows, units:].astype(F32)
            sigmoid_gate = jax.nn.sigmoid(gate_pre)
            grad_gate[rows, :] = (
                hidden_grad * up_pre * sigmoid_gate * (1.0 + gate_pre * (1.0 - sigmoid_gate))
            ).astype(BF16)
            grad_up[rows, :] = (hidden_grad * gate_pre * sigmoid_gate).astype(BF16)
        for copy in copies[2:]:
            copy.wait()

    columns = pl.ds(pl.multiple_of(step * width, 128), width)
    total = jnp.dot(grad_gate[...], gate[:, columns], preferred_element_type=F32)
    total = total + jnp.dot(grad_up[...], up[:, columns], preferred_element_type=F32)
    out_ref[...] = total.astype(BF16)


def expert_back(at, rows, saved, weights):
    width = 512
    units = saved[0].shape[1] // 2
    return pl.pallas_call(
        functools.partial(expert_kernel, parts=len(saved)),
        grid=(D // width,),
        in_specs=[SCALARS]
        + [pl.BlockSpec(memory_space=pltpu.HBM)] * (1 + len(saved))
        + [pl.BlockSpec(memory_space=pl.ANY)] * len(weights),
        out_specs=pl.BlockSpec((HALF_ROWS, width), lambda j: (0, j)),
        out_shape=pltpu.HBM((HALF_ROWS, D), BF16),
        scratch_shapes=[pltpu.VMEM((HALF_ROWS, D), BF16), pltpu.VMEM((HALF_ROWS, 2 * units), BF16)]
        + [pltpu.VMEM((units, D), BF16)] * 3
        + [pltpu.VMEM((HALF_ROWS, units), BF16)] * 2
        + [pltpu.SemaphoreType.DMA((7 + len(saved),))],
        compiler_params=pltpu.CompilerParams(vmem_limit_bytes=48 * MIB),
    )(at, rows, *saved, *weights)


def combine(collect, returned):
    return jnp.dot(collect, returned, preferred_element_type=F32).astype(BF16)


RING_STEPS = (4, 3, -3, 2, -2, 1, -1, 0)


def terms_kernel(at_ref, collect_hbm, back_hbm, own_hbm, *refs):
    outs, (collect, back, own, other, sems) = refs[: len(RING_STEPS)], refs[len(RING_STEPS) :]
    j = pl.program_id(0)
    width = other.shape[1]
    columns = pl.ds(pl.multiple_of(j * width, 128), width)
    arrivals = []
    for part in range(back_hbm.shape[1] // width):
        at_part = pl.ds(part * width, width)
        arrivals.append(
            pltpu.make_async_copy(back_hbm.at[:, at_part], back.at[:, at_part], sems.at[part])
        )
    others = [
        pltpu.make_async_copy(collect_hbm, collect, sems.at[len(arrivals)]),
        pltpu.make_async_copy(own_hbm, own, sems.at[len(arrivals) + 1]),
    ]

    @pl.when(j == 0)
    def _():
        for copy in (others[0], arrivals[0], others[1], *arrivals[1:]):
            copy.start()
        for copy in others:
            copy.wait()

    for part, copy in enumerate(arrivals):

        @pl.when(j == part)
        def _():
            copy.wait()

    other[...] = combine(collect[...], back[:, columns])
    for step, out in zip(RING_STEPS, outs):
        target = (at_ref[0] * 4 + at_ref[1] + step + RING) % RING
        rows = pl.ds(pl.multiple_of((target % 4) * TOK, TOK), TOK)
        out[...] = jnp.where(target // 4 == at_ref[0], own[rows, columns], other[rows, :])


def ring_terms(at, collect_other, back_other, terms_own):
    width = 512
    rows, slots = collect_other.shape
    outs = pl.pallas_call(
        terms_kernel,
        grid=(D // width,),
        in_specs=[SCALARS] + [pl.BlockSpec(memory_space=pltpu.HBM)] * 3,
        out_specs=[pl.BlockSpec((TOK, width), lambda j: (0, j))] * len(RING_STEPS),
        out_shape=[jax.ShapeDtypeStruct((TOK, D), BF16)] * len(RING_STEPS),
        scratch_shapes=[
            pltpu.VMEM((rows, slots), BF16),
            pltpu.VMEM((slots, D), BF16),
            pltpu.VMEM((rows, D), BF16),
            pltpu.VMEM((rows, width), BF16),
            pltpu.SemaphoreType.DMA((D // width + 2,)),
        ],
        compiler_params=pltpu.CompilerParams(vmem_limit_bytes=40 * MIB),
    )(at, collect_other, back_other, terms_own)
    return dict(zip(RING_STEPS, outs))


def own_features(value, core):
    a, b, c, d = (value[..., 256 * i : 256 * (i + 1)] for i in range(4))
    first = core == 0
    mine = jnp.concatenate([jnp.where(first, a, b), jnp.where(first, c, d)], axis=-1)
    theirs = jnp.concatenate([jnp.where(first, b, a), jnp.where(first, d, c)], axis=-1)
    return mine, theirs


def all_features(mine, theirs, core):
    first = core == 0
    low, high = slice(0, 256), slice(256, 512)
    return jnp.concatenate(
        [
            jnp.where(first, mine[:, low], theirs[:, low]),
            jnp.where(first, theirs[:, low], mine[:, low]),
            jnp.where(first, mine[:, high], theirs[:, high]),
            jnp.where(first, theirs[:, high], mine[:, high]),
        ],
        axis=1,
    )


def attention_kernel(
    at_ref,
    q_ref,
    k_ref,
    v_ref,
    near_hidden_ref,
    far_hidden_ref,
    near_weight_ref,
    far_weight_ref,
    mask_ref,
    dq_ref,
    dk_ref,
    dv_ref,
    far_ref,
    grads_ref,
):
    scale = 1.0 / math.sqrt(HD)
    here = q_ref.shape[0]
    head = pl.program_id(0)
    queries, keys, values = q_ref[...], k_ref[...], v_ref[...]
    last = (((1,), (1,)), ((), ()))
    rows_here = pl.ds(pl.multiple_of((head % 2) * HD, HD), HD)
    weight = jnp.where(
        head // 2 == at_ref[0], near_weight_ref[rows_here, :], far_weight_ref[rows_here, :]
    )
    for number, ref in enumerate((near_hidden_ref, far_hidden_ref)):
        grads_ref[number * TOK : (number + 1) * TOK, :] = lax.dot_general(
            ref[...], weight, last, preferred_element_type=F32
        ).astype(BF16)
    grads = grads_ref[...]
    rows = (((0,), (0,)), ((), ()))
    scores = lax.dot_general(queries, keys, last, preferred_element_type=F32) * scale
    scores = jnp.where(mask_ref[...] > 0.0, scores, -jnp.inf)
    expd = jnp.exp(scores - jnp.max(scores, axis=1, keepdims=True))
    probs = expd / jnp.sum(expd, axis=1, keepdims=True)
    probs_b = probs.astype(BF16)
    attn_out = jnp.dot(probs_b, values, preferred_element_type=F32)
    delta = jnp.sum(grads.astype(F32) * attn_out, axis=1, keepdims=True)
    dprobs = lax.dot_general(grads, values, last, preferred_element_type=F32)
    dscores = (probs * (dprobs - delta)).astype(BF16)
    dq_ref[...] = (jnp.dot(dscores, keys, preferred_element_type=F32) * scale).astype(BF16)
    grad_key = lax.dot_general(dscores, queries, rows, preferred_element_type=F32) * scale
    grad_value = lax.dot_general(probs_b, grads, rows, preferred_element_type=F32)
    dk_ref[...] = grad_key[:here]
    dv_ref[...] = grad_value[:here]
    far_ref[0] = grad_key[here:].astype(BF16)
    far_ref[1] = grad_value[here:].astype(BF16)


def attention_backward(at, queries, keys, values, hidden, weights, mask):
    here, features = queries.shape
    everywhere = keys.shape[0]
    heads = features // HD
    by_head = lambda rows: pl.BlockSpec((rows, HD), lambda h: (0, h))
    return pl.pallas_call(
        attention_kernel,
        grid=(heads,),
        in_specs=[SCALARS, by_head(here), by_head(everywhere), by_head(everywhere)]
        + [pl.BlockSpec(value.shape, lambda h: (0, 0)) for value in (*hidden, *weights, mask)],
        out_specs=[
            by_head(here),
            by_head(here),
            by_head(here),
            pl.BlockSpec((2, here, HD), lambda h: (0, 0, h)),
        ],
        out_shape=[
            jax.ShapeDtypeStruct((here, features), BF16),
            jax.ShapeDtypeStruct((here, features), F32),
            jax.ShapeDtypeStruct((here, features), F32),
            jax.ShapeDtypeStruct((2, here, features), BF16),
        ],
        scratch_shapes=[pltpu.VMEM((here, HD), BF16)],
        compiler_params=pltpu.CompilerParams(vmem_limit_bytes=32 * MIB),
    )(at, queries, keys, values, *hidden, *weights, mask)


def on_device(
    query,
    key_states,
    value_states,
    segment_ids,
    out_weight,
    grad_out,
    routes,
    route_gates,
    w_gate,
    w_up,
    w_down,
    saved_gate,
    saved_up,
):
    z_high, core, z_low = lax.axis_index("zh"), lax.axis_index("core"), lax.axis_index("zl")
    tokens = grad_out[0]

    at = jnp.stack([z_high, z_low, core]).astype(jnp.int32)

    half = TOK // 2
    blocks = {0: tokens}
    blocks[1], blocks[-1] = ring_shift(tokens, -1), ring_shift(tokens, 1)
    segment_chip = jnp.concatenate([segment_ids, swap(segment_ids, "core")], axis=0)
    table = route_table(routes, route_gates, segment_chip)
    saved_own, saved_leaving = split_saved(at, saved_gate[0], saved_up[0])
    blocks[1], blocks[-1], table, at, saved_leaving = together(
        blocks[1], blocks[-1], table, at, saved_leaving
    )

    blocks[2], blocks[-2] = ring_shift(blocks[1], -1), ring_shift(blocks[-1], 1)
    tables = lax.all_to_all(
        jnp.broadcast_to(table[None], (RING, 16, TOK)), RING_AXES, 0, 0, tiled=True
    )
    blocks[2], blocks[-2], tables, at = together(blocks[2], blocks[-2], tables, at)

    blocks[3], blocks[-3] = ring_shift(blocks[2], -1), ring_shift(blocks[-2], 1)
    place_own, place_other = placement(at, tables)
    blocks[3], blocks[-3], place_own, place_other, at = together(
        blocks[3], blocks[-3], place_own, place_other, at
    )
    select_own, collect_own, gate_own = place_own
    select_other, collect_other, gate_other = place_other

    last_up, last_down = ring_shift(blocks[3][:half], -1), ring_shift(blocks[-3][half:], 1)
    leaving_rows = dispatch(at, select_own, gate_own, [blocks[i] for i in NEAR])
    last_up, last_down, saved_leaving, leaving_rows, at = together(
        last_up, last_down, saved_leaving, leaving_rows, at
    )
    blocks[4] = jnp.concatenate([last_up, last_down], axis=0)

    rows_own = plane_exchange(leaving_rows)
    saved_other = [swap(saved_leaving[0], "zh")]
    leaving_rows = dispatch(at, select_other, gate_other, [blocks[i] for i in FAR])
    core_here, _ = together(core, last_up)
    heads_mine, heads_theirs = [], []
    for value in (query[0], key_states[0], value_states[0]):
        mine, theirs = own_features(value, core_here)
        heads_mine.append(mine)
        heads_theirs.append(theirs)
    arriving = swap(jnp.concatenate(heads_theirs, axis=1), "core")
    queries = jnp.concatenate([heads_mine[0], arriving[:, :512]], axis=0)
    key_value = jnp.concatenate(
        [jnp.concatenate(heads_mine[1:], axis=1), arriving[:, 512:]], axis=0
    )
    (
        rows_own,
        leaving_rows,
        saved_own,
        saved_other[0],
        saved_next,
        queries,
        key_value,
    ) = together(
        rows_own,
        leaving_rows,
        saved_own,
        saved_other[0],
        saved_leaving[1],
        queries,
        key_value,
    )

    rows_other = plane_exchange(leaving_rows)
    saved_other.append(swap(saved_next, "zh"))
    weights = []
    for weight in (w_down, w_gate, w_up):
        piece = jnp.swapaxes(weight[0], 0, 1)
        weights += [piece, swap(piece, "core")]
    leaving_own = expert_back(at, rows_own, [saved_own], weights)
    (
        rows_other,
        leaving_own,
        saved_other[1],
        saved_next,
        key_value,
    ) = together(
        rows_other,
        leaving_own,
        saved_other[1],
        saved_leaving[2],
        key_value,
    )

    back_own = plane_exchange(leaving_own)
    saved_other.append(swap(saved_next, "zh"))
    strip = out_weight.shape[0] // 4
    own_strip = lax.dynamic_slice_in_dim(out_weight, lax.axis_index("x") * strip, strip, axis=0)
    leaving = expert_back(at, rows_other, saved_other, weights)
    back_own, leaving, own_strip, key_value = together(back_own, leaving, own_strip, key_value)

    back_other = plane_exchange(leaving)
    key_value_far = swap(key_value, "zh")
    terms_own = combine(collect_own, back_own)
    table_far = lax.dynamic_index_in_dim(tables, (1 - z_high) * 4 + z_low, 0, keepdims=False)
    segment_keys = jnp.concatenate([table[8:10], table_far[8:10]], axis=0)
    segment_keys = segment_keys.astype(jnp.int32).reshape(4 * TOK)
    fetched = swap(own_strip, "zh")
    back_other, terms_own, key_value_far, segment_keys, fetched = together(
        back_other, terms_own, key_value_far, segment_keys, fetched
    )

    terms = ring_terms(at, collect_other, back_other, terms_own)
    middle = D // 2
    up = ring_shift(terms[4][:, :middle], 1)
    down = ring_shift(terms[4][:, middle:], -1)
    up, down, fetched, key_value, key_value_far, segment_keys = together(
        up, down, fetched, key_value, key_value_far, segment_keys
    )
    terms = {step: value.astype(F32) for step, value in terms.items()}
    ahead, behind = terms[3], terms[-3]
    ahead = jnp.concatenate([ahead[:, :middle] + up.astype(F32), ahead[:, middle:]], axis=1)
    behind = jnp.concatenate([behind[:, :middle], behind[:, middle:] + down.astype(F32)], axis=1)
    for step in (2, 1, 0):
        ahead, behind = together(ahead.astype(BF16), behind.astype(BF16))
        up, down = ring_shift(ahead, 1), ring_shift(behind, -1)
        if step == 2:
            keys = jnp.concatenate([key_value[:, :512], key_value_far[:, :512]], axis=0)
            values = jnp.concatenate([key_value[:, 512:], key_value_far[:, 512:]], axis=0)
            offsets = jnp.arange(TOK, dtype=jnp.int32)
            place = lambda high, which: (high * 2 + which) * TOK + offsets
            chip_place = jnp.concatenate([place(z_high, core), place(z_high, 1 - core)])
            key_place = jnp.concatenate([chip_place, place(1 - z_high, core), place(1 - z_high, 1 - core)])
            segment_here = segment_keys[: 2 * TOK, None]
            causal = key_place[None, :] <= chip_place[:, None]
            image = (segment_here == segment_keys[None, :]) & (segment_here % 2 == 1)
            mask = (causal | image).astype(F32)
            pieces = [fetched]
            for distance in (1, 2, 3):
                pieces.append(lax.ppermute(fetched, "x", [((i + distance) % 4, i) for i in range(4)]))
            up, down, keys, values, mask, pieces = together(up, down, keys, values, mask, pieces)
        elif step == 1:
            weight_far = lax.dynamic_slice_in_dim(
                jnp.concatenate(pieces + pieces[:3], axis=0),
                (4 - lax.axis_index("x")) % 4 * strip,
                4 * strip,
                axis=0,
            )
            up, down, weight_far = together(up, down, weight_far)
        else:
            up, down = together(up, down)
        if step > 0:
            ahead = terms[step] + up.astype(F32)
            behind = terms[-step] + down.astype(F32)
    summed = tokens.astype(F32) + terms[0] + up.astype(F32) + down.astype(F32)
    d_hidden = summed.astype(BF16)

    grad_query, grad_key, grad_value, far = attention_backward(
        at,
        queries,
        keys,
        values,
        (d_hidden, swap(d_hidden, "core")),
        (out_weight, weight_far),
        mask,
    )
    far_theirs = swap(far[:, TOK:], "core")
    far_full = jnp.stack([all_features(far[i, :TOK], far_theirs[i], core) for i in range(2)])
    arrived = swap(far_full, "zh").astype(F32)
    near = [
        all_features(grad[:TOK], swap(grad[TOK:], "core"), core)
        for grad in (grad_query, grad_key, grad_value)
    ]
    return (
        d_hidden[None],
        near[0][None],
        (near[1] + arrived[0]).astype(BF16)[None],
        (near[2] + arrived[1]).astype(BF16)[None],
    )


def solution(mesh):
    fine = Mesh(mesh.devices.reshape(2, 2, 4, 4, 4), ("zh", "core", "x", "y", "zl"))
    exp = ("x", "y", "zl")
    ctx = ("zh", "core")
    in_specs = (
        P(exp, ctx, None),
        P(exp, ctx, None),
        P(exp, ctx, None),
        P(exp, ctx),
        P(ctx, None),
        P(exp, ctx, None),
        P(exp, ctx, None),
        P(exp, ctx, None),
        P(exp, None, ctx),
        P(exp, None, ctx),
        P(exp, None, ctx),
        P(exp, ctx, None),
        P(exp, ctx, None),
    )
    out_specs = (P(exp, ctx, None),) * 4
    return jax.shard_map(
        on_device, mesh=fine, in_specs=in_specs, out_specs=out_specs, check_vma=False
    )
```

```python
import functools
import math

import jax
import jax.numpy as jnp
from jax import lax
from jax.experimental import pallas as pl
from jax.experimental.pallas import tpu as pltpu
from jax.sharding import Mesh
from jax.sharding import PartitionSpec as P

D = 2048
HEADS = 8
HD = 128
EXPERTS = 64
CAP = 10
TOK = 128
RING = 8
RING_AXES = ("zh", "zl")
PLANE_AXES = ("x", "y")
PLANE = 16
HALF_ROWS = EXPERTS * CAP
F32 = jnp.float32
BF16 = jnp.bfloat16


def ring_shift(value, step):
    return lax.ppermute(value, RING_AXES, [(i, (i + step) % RING) for i in range(RING)])


def swap(value, axis):
    return lax.ppermute(value, axis, [(0, 1), (1, 0)])


def plane_exchange(rows):
    width = rows.shape[1]
    return lax.all_to_all(
        rows.reshape(PLANE, HALF_ROWS // PLANE, width), PLANE_AXES, 0, 0, tiled=True
    ).reshape(HALF_ROWS, width)


def together(*values):
    return lax.optimization_barrier(values)


def route_table(routes, route_gates, segments):
    ids = routes[0]
    experts = jnp.arange(EXPERTS, dtype=jnp.int32)
    named = (ids[:, :, None] == experts).astype(F32)
    table = jnp.sum(named, axis=1)
    position = jnp.arange(TOK, dtype=jnp.int32)
    earlier = (position[None, :] < position[:, None]).astype(BF16)
    before = jnp.dot(earlier, table.astype(BF16), preferred_element_type=F32)
    slot = jnp.sum(named * before[:, None, :], axis=2)
    codes = ids.astype(F32) * 16.0 + slot
    spare = jnp.zeros((6, TOK), F32)
    return jnp.concatenate([codes.T, route_gates[0].T, segments.astype(F32), spare], axis=0)


NEAR = (-3, -2, -1, 0, 1, 2, 3)
FAR = (1, 2, 3, 4, -3, -2, -1)
SAVED_ROWS = (256, 256, 128)
SAVED_BLOCK = 128
MIB = 1024 * 1024


SCALARS = pl.BlockSpec(memory_space=pltpu.SMEM)


def saved_kernel(at_ref, gate_ref, up_ref, own_ref, *outs):
    units = gate_ref.shape[1] // 2
    step = pl.program_id(0)
    first = 0
    for high in range(2):

        @pl.when(at_ref[0] == high)
        def _():
            mine = slice(high * units, (high + 1) * units)
            own_ref[:, :units] = gate_ref[:, mine]
            own_ref[:, units:] = up_ref[:, mine]

    for ref, rows in zip(outs, SAVED_ROWS):
        for high in range(2):

            @pl.when((at_ref[0] == high) & (step >= first) & (step < first + rows // SAVED_BLOCK))
            def _():
                other = slice((1 - high) * units, (2 - high) * units)
                ref[:, :units] = gate_ref[:, other]
                ref[:, units:] = up_ref[:, other]

        first += rows // SAVED_BLOCK


def split_saved(at, saved_gate, saved_up):
    width = saved_gate.shape[1]
    by_rows = pl.BlockSpec((SAVED_BLOCK, width), lambda i: (i, 0))
    parts, shapes, first = [], [], 0
    for rows in SAVED_ROWS:
        count = rows // SAVED_BLOCK
        parts.append(
            pl.BlockSpec(
                (SAVED_BLOCK, width),
                lambda i, first=first, count=count: (jnp.clip(i - first, 0, count - 1), 0),
            )
        )
        shapes.append(jax.ShapeDtypeStruct((rows, width), BF16))
        first += count
    own, *other = pl.pallas_call(
        saved_kernel,
        grid=(HALF_ROWS // SAVED_BLOCK,),
        in_specs=[SCALARS, by_rows, by_rows],
        out_specs=[by_rows, *parts],
        out_shape=[jax.ShapeDtypeStruct(saved_gate.shape, BF16), *shapes],
        compiler_params=pltpu.CompilerParams(vmem_limit_bytes=24 * MIB),
    )(at, saved_gate, saved_up)
    return own, other


def placement_kernel(at_ref, tables_ref, *outs):
    numbers = lax.broadcasted_iota(jnp.int32, (HALF_ROWS, TOK), 0)
    for which in range(2):
        select_ref, collect_ref, gate_ref = outs[3 * which : 3 * which + 3]
        first = 4 * (at_ref[0] if which == 0 else 1 - at_ref[0])
        total = jnp.zeros((HALF_ROWS, 1), F32)
        for source in range(4):
            table = tables_ref[first + source]
            codes = table[:4].astype(jnp.int32)
            expert = codes >> 4
            row = (expert >> 2) * (4 * CAP) + source * CAP + (codes & 15)
            row = jnp.where((expert & 3) == at_ref[1], row, -1)
            marks = jnp.zeros((HALF_ROWS, TOK), F32)
            gates = jnp.zeros((HALF_ROWS, TOK), F32)
            for choice in range(4):
                hit = numbers == row[choice : choice + 1]
                marks = jnp.where(hit, 1.0, marks)
                gates = jnp.where(hit, table[4 + choice : 5 + choice], gates)
            columns = slice(source * TOK, (source + 1) * TOK)
            select_ref[:, columns] = marks.astype(BF16)
            collect_ref[columns, :] = marks.T.astype(BF16)
            total = total + jnp.sum(gates, axis=1, keepdims=True)
        gate_ref[...] = total


def placement(at, tables):
    shapes = [
        jax.ShapeDtypeStruct((HALF_ROWS, 4 * TOK), BF16),
        jax.ShapeDtypeStruct((4 * TOK, HALF_ROWS), BF16),
        jax.ShapeDtypeStruct((HALF_ROWS, 1), F32),
    ] * 2
    outs = pl.pallas_call(
        placement_kernel,
        grid=(1,),
        in_specs=[SCALARS, pl.BlockSpec(tables.shape, lambda j: (0, 0, 0))],
        out_specs=[pl.BlockSpec(shape.shape, lambda j: (0, 0)) for shape in shapes],
        out_shape=shapes,
        compiler_params=pltpu.CompilerParams(vmem_limit_bytes=24 * MIB),
    )(at, tables)
    return outs[:3], outs[3:]


def dispatch_kernel(at_ref, select_ref, gate_ref, *refs):
    blocks, rows_ref, tokens = refs[:7], refs[7], refs[8]
    for low in range(4):

        @pl.when(at_ref[1] == low)
        def _():
            for source in range(4):
                tokens[source * TOK : (source + 1) * TOK, :] = blocks[source + 3 - low][...]

    picked = jnp.dot(select_ref[...], tokens[...], preferred_element_type=F32)
    rows_ref[...] = (picked * gate_ref[...]).astype(BF16)


def dispatch(at, select, row_gate, blocks):
    width = 512
    return pl.pallas_call(
        dispatch_kernel,
        grid=(D // width,),
        in_specs=[
            SCALARS,
            pl.BlockSpec(select.shape, lambda j: (0, 0)),
            pl.BlockSpec(row_gate.shape, lambda j: (0, 0)),
        ]
        + [pl.BlockSpec((TOK, width), lambda j: (0, j))] * 7,
        out_specs=pl.BlockSpec((HALF_ROWS, width), lambda j: (0, j)),
        out_shape=pltpu.HBM((HALF_ROWS, D), BF16),
        scratch_shapes=[pltpu.VMEM((4 * TOK, width), BF16)],
        compiler_params=pltpu.CompilerParams(vmem_limit_bytes=40 * MIB),
    )(at, select, row_gate, *blocks)


def expert_kernel(at_ref, *refs, parts):
    rows_hbm, saved_hbm = refs[0], refs[1 : 1 + parts]
    weights, refs = refs[1 + parts : 7 + parts], refs[7 + parts :]
    out_ref, rows_ref, saved, down, gate, up, grad_gate, grad_up, sems = refs
    piece = weights[0].shape[0]
    units = 2 * piece
    step = pl.program_id(0)
    width = out_ref.shape[1]

    @pl.when(step == 0)
    def _():
        copies = []
        for number, ref in enumerate(weights):
            where = at_ref[2] if number % 2 == 0 else 1 - at_ref[2]
            start = pl.multiple_of(where * piece, 16)
            target = (down, gate, up)[number // 2].at[pl.ds(start, piece), :]
            copies.append(pltpu.make_async_copy(ref, target, sems.at[number]))
        needed = [pltpu.make_async_copy(rows_hbm, rows_ref, sems.at[6])]
        first = 0
        for number, ref in enumerate(saved_hbm):
            target = saved.at[pl.ds(first, ref.shape[0]), :]
            needed.append(pltpu.make_async_copy(ref, target, sems.at[7 + number]))
            first += ref.shape[0]
        for copy in (*copies[:2], *needed, *copies[2:]):
            copy.start()
        for copy in (*copies[:2], *needed):
            copy.wait()
        for first in range(0, HALF_ROWS, 320):
            rows = slice(first, first + 320)
            hidden_grad = lax.dot_general(
                rows_ref[rows, :],
                down[...],
                (((1,), (1,)), ((), ())),
                preferred_element_type=F32,
            )
            gate_pre = saved[rows, :units].astype(F32)
            up_pre = saved[rows, units:].astype(F32)
            sigmoid_gate = jax.nn.sigmoid(gate_pre)
            grad_gate[rows, :] = (
                hidden_grad * up_pre * sigmoid_gate * (1.0 + gate_pre * (1.0 - sigmoid_gate))
            ).astype(BF16)
            grad_up[rows, :] = (hidden_grad * gate_pre * sigmoid_gate).astype(BF16)
        for copy in copies[2:]:
            copy.wait()

    columns = pl.ds(pl.multiple_of(step * width, 128), width)
    total = jnp.dot(grad_gate[...], gate[:, columns], preferred_element_type=F32)
    total = total + jnp.dot(grad_up[...], up[:, columns], preferred_element_type=F32)
    out_ref[...] = total.astype(BF16)


def expert_back(at, rows, saved, weights):
    width = 512
    units = saved[0].shape[1] // 2
    return pl.pallas_call(
        functools.partial(expert_kernel, parts=len(saved)),
        grid=(D // width,),
        in_specs=[SCALARS]
        + [pl.BlockSpec(memory_space=pltpu.HBM)] * (1 + len(saved))
        + [pl.BlockSpec(memory_space=pl.ANY)] * len(weights),
        out_specs=pl.BlockSpec((HALF_ROWS, width), lambda j: (0, j)),
        out_shape=pltpu.HBM((HALF_ROWS, D), BF16),
        scratch_shapes=[pltpu.VMEM((HALF_ROWS, D), BF16), pltpu.VMEM((HALF_ROWS, 2 * units), BF16)]
        + [pltpu.VMEM((units, D), BF16)] * 3
        + [pltpu.VMEM((HALF_ROWS, units), BF16)] * 2
        + [pltpu.SemaphoreType.DMA((7 + len(saved),))],
        compiler_params=pltpu.CompilerParams(vmem_limit_bytes=48 * MIB),
    )(at, rows, *saved, *weights)


def combine(collect, returned):
    return jnp.dot(collect, returned, preferred_element_type=F32).astype(BF16)


RING_STEPS = (4, 3, -3, 2, -2, 1, -1, 0)


def terms_kernel(at_ref, collect_hbm, back_hbm, own_hbm, *refs):
    outs, (collect, back, own, other, sems) = refs[: len(RING_STEPS)], refs[len(RING_STEPS) :]
    j = pl.program_id(0)
    width = other.shape[1]
    columns = pl.ds(pl.multiple_of(j * width, 128), width)
    arrivals = []
    for part in range(back_hbm.shape[1] // width):
        at_part = pl.ds(part * width, width)
        arrivals.append(
            pltpu.make_async_copy(back_hbm.at[:, at_part], back.at[:, at_part], sems.at[part])
        )
    others = [
        pltpu.make_async_copy(collect_hbm, collect, sems.at[len(arrivals)]),
        pltpu.make_async_copy(own_hbm, own, sems.at[len(arrivals) + 1]),
    ]

    @pl.when(j == 0)
    def _():
        for copy in (others[0], arrivals[0], others[1], *arrivals[1:]):
            copy.start()
        for copy in others:
            copy.wait()

    for part, copy in enumerate(arrivals):

        @pl.when(j == part)
        def _():
            copy.wait()

    other[...] = combine(collect[...], back[:, columns])
    for step, out in zip(RING_STEPS, outs):
        target = (at_ref[0] * 4 + at_ref[1] + step + RING) % RING
        rows = pl.ds(pl.multiple_of((target % 4) * TOK, TOK), TOK)
        out[...] = jnp.where(target // 4 == at_ref[0], own[rows, columns], other[rows, :])


def ring_terms(at, collect_other, back_other, terms_own):
    width = 512
    rows, slots = collect_other.shape
    outs = pl.pallas_call(
        terms_kernel,
        grid=(D // width,),
        in_specs=[SCALARS] + [pl.BlockSpec(memory_space=pltpu.HBM)] * 3,
        out_specs=[pl.BlockSpec((TOK, width), lambda j: (0, j))] * len(RING_STEPS),
        out_shape=[jax.ShapeDtypeStruct((TOK, D), BF16)] * len(RING_STEPS),
        scratch_shapes=[
            pltpu.VMEM((rows, slots), BF16),
            pltpu.VMEM((slots, D), BF16),
            pltpu.VMEM((rows, D), BF16),
            pltpu.VMEM((rows, width), BF16),
            pltpu.SemaphoreType.DMA((D // width + 2,)),
        ],
        compiler_params=pltpu.CompilerParams(vmem_limit_bytes=40 * MIB),
    )(at, collect_other, back_other, terms_own)
    return dict(zip(RING_STEPS, outs))


def own_features(value, core):
    a, b, c, d = (value[..., 256 * i : 256 * (i + 1)] for i in range(4))
    first = core == 0
    mine = jnp.concatenate([jnp.where(first, a, b), jnp.where(first, c, d)], axis=-1)
    theirs = jnp.concatenate([jnp.where(first, b, a), jnp.where(first, d, c)], axis=-1)
    return mine, theirs


def all_features(mine, theirs, core):
    first = core == 0
    low, high = slice(0, 256), slice(256, 512)
    return jnp.concatenate(
        [
            jnp.where(first, mine[:, low], theirs[:, low]),
            jnp.where(first, theirs[:, low], mine[:, low]),
            jnp.where(first, mine[:, high], theirs[:, high]),
            jnp.where(first, theirs[:, high], mine[:, high]),
        ],
        axis=1,
    )


def attention_kernel(
    at_ref,
    q_ref,
    k_ref,
    v_ref,
    near_hidden_ref,
    far_hidden_ref,
    near_weight_ref,
    far_weight_ref,
    mask_ref,
    dq_ref,
    dk_ref,
    dv_ref,
    far_ref,
    grads_ref,
):
    scale = 1.0 / math.sqrt(HD)
    here = q_ref.shape[0]
    head = pl.program_id(0)
    queries, keys, values = q_ref[...], k_ref[...], v_ref[...]
    last = (((1,), (1,)), ((), ()))
    rows_here = pl.ds(pl.multiple_of((head % 2) * HD, HD), HD)
    weight = jnp.where(
        head // 2 == at_ref[0], near_weight_ref[rows_here, :], far_weight_ref[rows_here, :]
    )
    for number, ref in enumerate((near_hidden_ref, far_hidden_ref)):
        grads_ref[number * TOK : (number + 1) * TOK, :] = lax.dot_general(
            ref[...], weight, last, preferred_element_type=F32
        ).astype(BF16)
    grads = grads_ref[...]
    rows = (((0,), (0,)), ((), ()))
    scores = lax.dot_general(queries, keys, last, preferred_element_type=F32) * scale
    scores = jnp.where(mask_ref[...] > 0.0, scores, -jnp.inf)
    expd = jnp.exp(scores - jnp.max(scores, axis=1, keepdims=True))
    probs = expd / jnp.sum(expd, axis=1, keepdims=True)
    probs_b = probs.astype(BF16)
    attn_out = jnp.dot(probs_b, values, preferred_element_type=F32)
    delta = jnp.sum(grads.astype(F32) * attn_out, axis=1, keepdims=True)
    dprobs = lax.dot_general(grads, values, last, preferred_element_type=F32)
    dscores = (probs * (dprobs - delta)).astype(BF16)
    dq_ref[...] = (jnp.dot(dscores, keys, preferred_element_type=F32) * scale).astype(BF16)
    grad_key = lax.dot_general(dscores, queries, rows, preferred_element_type=F32) * scale
    grad_value = lax.dot_general(probs_b, grads, rows, preferred_element_type=F32)
    dk_ref[...] = grad_key[:here]
    dv_ref[...] = grad_value[:here]
    far_ref[0] = grad_key[here:].astype(BF16)
    far_ref[1] = grad_value[here:].astype(BF16)


def attention_backward(at, queries, keys, values, hidden, weights, mask):
    here, features = queries.shape
    everywhere = keys.shape[0]
    heads = features // HD
    by_head = lambda rows: pl.BlockSpec((rows, HD), lambda h: (0, h))
    return pl.pallas_call(
        attention_kernel,
        grid=(heads,),
        in_specs=[SCALARS, by_head(here), by_head(everywhere), by_head(everywhere)]
        + [pl.BlockSpec(value.shape, lambda h: (0, 0)) for value in (*hidden, *weights, mask)],
        out_specs=[
            by_head(here),
            by_head(here),
            by_head(here),
            pl.BlockSpec((2, here, HD), lambda h: (0, 0, h)),
        ],
        out_shape=[
            jax.ShapeDtypeStruct((here, features), BF16),
            jax.ShapeDtypeStruct((here, features), F32),
            jax.ShapeDtypeStruct((here, features), F32),
            jax.ShapeDtypeStruct((2, here, features), BF16),
        ],
        scratch_shapes=[pltpu.VMEM((here, HD), BF16)],
        compiler_params=pltpu.CompilerParams(vmem_limit_bytes=32 * MIB),
    )(at, queries, keys, values, *hidden, *weights, mask)


def on_device(
    query,
    key_states,
    value_states,
    segment_ids,
    out_weight,
    grad_out,
    routes,
    route_gates,
    w_gate,
    w_up,
    w_down,
    saved_gate,
    saved_up,
):
    z_high, core, z_low = lax.axis_index("zh"), lax.axis_index("core"), lax.axis_index("zl")
    tokens = grad_out[0]

    at = jnp.stack([z_high, z_low, core]).astype(jnp.int32)

    half = TOK // 2
    blocks = {0: tokens}
    blocks[1], blocks[-1] = ring_shift(tokens, -1), ring_shift(tokens, 1)
    segment_chip = jnp.concatenate([segment_ids, swap(segment_ids, "core")], axis=0)
    table = route_table(routes, route_gates, segment_chip)
    saved_own, saved_leaving = split_saved(at, saved_gate[0], saved_up[0])
    blocks[1], blocks[-1], table, at, saved_leaving = together(
        blocks[1], blocks[-1], table, at, saved_leaving
    )

    blocks[2], blocks[-2] = ring_shift(blocks[1], -1), ring_shift(blocks[-1], 1)
    tables = lax.all_to_all(
        jnp.broadcast_to(table[None], (RING, 16, TOK)), RING_AXES, 0, 0, tiled=True
    )
    blocks[2], blocks[-2], tables, at = together(blocks[2], blocks[-2], tables, at)

    blocks[3], blocks[-3] = ring_shift(blocks[2], -1), ring_shift(blocks[-2], 1)
    place_own, place_other = placement(at, tables)
    blocks[3], blocks[-3], place_own, place_other, at = together(
        blocks[3], blocks[-3], place_own, place_other, at
    )
    select_own, collect_own, gate_own = place_own
    select_other, collect_other, gate_other = place_other

    last_up, last_down = ring_shift(blocks[3][:half], -1), ring_shift(blocks[-3][half:], 1)
    leaving_rows = dispatch(at, select_own, gate_own, [blocks[i] for i in NEAR])
    last_up, last_down, saved_leaving, leaving_rows, at = together(
        last_up, last_down, saved_leaving, leaving_rows, at
    )
    blocks[4] = jnp.concatenate([last_up, last_down], axis=0)

    rows_own = plane_exchange(leaving_rows)
    saved_other = [swap(saved_leaving[0], "zh")]
    leaving_rows = dispatch(at, select_other, gate_other, [blocks[i] for i in FAR])
    core_here, _ = together(core, last_up)
    heads_mine, heads_theirs = [], []
    for value in (query[0], key_states[0], value_states[0]):
        mine, theirs = own_features(value, core_here)
        heads_mine.append(mine)
        heads_theirs.append(theirs)
    arriving = swap(jnp.concatenate(heads_theirs, axis=1), "core")
    queries = jnp.concatenate([heads_mine[0], arriving[:, :512]], axis=0)
    key_value = jnp.concatenate(
        [jnp.concatenate(heads_mine[1:], axis=1), arriving[:, 512:]], axis=0
    )
    (
        rows_own,
        leaving_rows,
        saved_own,
        saved_other[0],
        saved_next,
        queries,
        key_value,
    ) = together(
        rows_own,
        leaving_rows,
        saved_own,
        saved_other[0],
        saved_leaving[1],
        queries,
        key_value,
    )

    rows_other = plane_exchange(leaving_rows)
    saved_other.append(swap(saved_next, "zh"))
    weights = []
    for weight in (w_down, w_gate, w_up):
        piece = jnp.swapaxes(weight[0], 0, 1)
        weights += [piece, swap(piece, "core")]
    leaving_own = expert_back(at, rows_own, [saved_own], weights)
    (
        rows_other,
        leaving_own,
        saved_other[1],
        saved_next,
        key_value,
    ) = together(
        rows_other,
        leaving_own,
        saved_other[1],
        saved_leaving[2],
        key_value,
    )

    back_own = plane_exchange(leaving_own)
    saved_other.append(swap(saved_next, "zh"))
    strip = out_weight.shape[0] // 4
    own_strip = lax.dynamic_slice_in_dim(out_weight, lax.axis_index("x") * strip, strip, axis=0)
    leaving = expert_back(at, rows_other, saved_other, weights)
    back_own, leaving, own_strip, key_value = together(back_own, leaving, own_strip, key_value)

    back_other = plane_exchange(leaving)
    key_value_far = swap(key_value, "zh")
    terms_own = combine(collect_own, back_own)
    table_far = lax.dynamic_index_in_dim(tables, (1 - z_high) * 4 + z_low, 0, keepdims=False)
    segment_keys = jnp.concatenate([table[8:10], table_far[8:10]], axis=0)
    segment_keys = segment_keys.astype(jnp.int32).reshape(4 * TOK)
    fetched = swap(own_strip, "zh")
    back_other, terms_own, key_value_far, segment_keys, fetched = together(
        back_other, terms_own, key_value_far, segment_keys, fetched
    )

    terms = ring_terms(at, collect_other, back_other, terms_own)
    terms[4], fetched, key_value_far, segment_keys = together(
        terms[4], fetched, key_value_far, segment_keys
    )
    middle = D // 2
    up = ring_shift(terms[4][:, :middle], 1)
    down = ring_shift(terms[4][:, middle:], -1)
    keys = jnp.concatenate([key_value[:, :512], key_value_far[:, :512]], axis=0)
    values = jnp.concatenate([key_value[:, 512:], key_value_far[:, 512:]], axis=0)
    offsets = jnp.arange(TOK, dtype=jnp.int32)
    place = lambda high, which: (high * 2 + which) * TOK + offsets
    chip_place = jnp.concatenate([place(z_high, core), place(z_high, 1 - core)])
    key_place = jnp.concatenate([chip_place, place(1 - z_high, core), place(1 - z_high, 1 - core)])
    segment_here = segment_keys[: 2 * TOK, None]
    causal = key_place[None, :] <= chip_place[:, None]
    image = (segment_here == segment_keys[None, :]) & (segment_here % 2 == 1)
    mask = (causal | image).astype(F32)
    pieces = [fetched]
    for distance in (1, 2, 3):
        pieces.append(lax.ppermute(fetched, "x", [((i + distance) % 4, i) for i in range(4)]))
    weight_far = lax.dynamic_slice_in_dim(
        jnp.concatenate(pieces + pieces[:3], axis=0),
        (4 - lax.axis_index("x")) % 4 * strip,
        4 * strip,
        axis=0,
    )
    up, down, keys, values, mask, weight_far = together(
        up, down, keys, values, mask, weight_far
    )
    terms = {step: value.astype(F32) for step, value in terms.items()}
    ahead, behind = terms[3], terms[-3]
    ahead = jnp.concatenate([ahead[:, :middle] + up.astype(F32), ahead[:, middle:]], axis=1)
    behind = jnp.concatenate([behind[:, :middle], behind[:, middle:] + down.astype(F32)], axis=1)
    for step in (2, 1, 0):
        ahead, behind = together(ahead.astype(BF16), behind.astype(BF16))
        up, down = together(ring_shift(ahead, 1), ring_shift(behind, -1))
        if step > 0:
            ahead = terms[step] + up.astype(F32)
            behind = terms[-step] + down.astype(F32)
    summed = tokens.astype(F32) + terms[0] + up.astype(F32) + down.astype(F32)
    d_hidden = summed.astype(BF16)

    grad_query, grad_key, grad_value, far = attention_backward(
        at,
        queries,
        keys,
        values,
        (d_hidden, swap(d_hidden, "core")),
        (out_weight, weight_far),
        mask,
    )
    far_theirs = swap(far[:, TOK:], "core")
    far_full = jnp.stack([all_features(far[i, :TOK], far_theirs[i], core) for i in range(2)])
    arrived = swap(far_full, "zh").astype(F32)
    near = [
        all_features(grad[:TOK], swap(grad[TOK:], "core"), core)
        for grad in (grad_query, grad_key, grad_value)
    ]
    return (
        d_hidden[None],
        near[0][None],
        (near[1] + arrived[0]).astype(BF16)[None],
        (near[2] + arrived[1]).astype(BF16)[None],
    )


def solution(mesh):
    fine = Mesh(mesh.devices.reshape(2, 2, 4, 4, 4), ("zh", "core", "x", "y", "zl"))
    exp = ("x", "y", "zl")
    ctx = ("zh", "core")
    in_specs = (
        P(exp, ctx, None),
        P(exp, ctx, None),
        P(exp, ctx, None),
        P(exp, ctx),
        P(ctx, None),
        P(exp, ctx, None),
        P(exp, ctx, None),
        P(exp, ctx, None),
        P(exp, None, ctx),
        P(exp, None, ctx),
        P(exp, None, ctx),
        P(exp, ctx, None),
        P(exp, ctx, None),
    )
    out_specs = (P(exp, ctx, None),) * 4
    return jax.shard_map(
        on_device, mesh=fine, in_specs=in_specs, out_specs=out_specs, check_vma=False
    )
```
